128 devices in a mesh: dp: 32 (over y, x, core), seq: 4 (over z).
Axes of the slice: x: 4, y: 4, z: 4, core: 2. Of those that a mesh axis runs over, the one named last changes fastest.
Arguments:
- token_rows: bfloat16 [163840, 5120], P(('dp', 'seq')), may hold values from -6 to 6
- key_rows: bfloat16 [163840, 128], P(('dp', 'seq')), may hold values from -1.8 to 1.8
- query_rows: bfloat16 [163840, 128], P(('dp', 'seq')), may hold values from -0.1796875 to 0.1796875
- step_rows: bfloat16 [163840, 80], P(('dp', 'seq')), may hold values from -6 to 1000
- decay_log: float32 [80], replicated, may hold values from -9.3 to -1.8
- skip_gain: float32 [80], replicated, may hold values from 0.5 to 1.5
- source_rows: int32 [32, 5120], P('dp', 'seq'), may hold values from 0 to 163839, as said below
- document_starts: int32 [32, 6], P('dp'), may hold values from 0 to 5119, as said below
Outputs:
- layer_result_rows: bfloat16 [32, 5120, 5120], P('dp', 'seq')
The draws below stay inside these ranges and needn't reach their ends.
Inputs may be any that keep to these rules, and one draw needn't show every extreme that they name: `source_rows`: every loaded row is placed exactly once. The row at position p of a packed sequence is held by a device whose seq index is p // 1280. Positions come in aligned runs of 8 that hold consecutive rows of one device. A device takes at most 48 of its positions from any one device, and in every seq index some pair of devices reaches that number. `document_starts`: each row is strictly increasing and begins with 0.
All inputs are finite; a program needn't handle non-finite values.
Results may differ from the reference program's by a relative error of at most 0.0065.
Values may be sent and summed in bfloat16 or wider, within the bound.
No kernel may reach another device: no remote copies, remote signals or barrier semaphores. Data moves between devices by JAX's collectives and lax.ppermute only.
A program may use at most 192 MiB of HBM per device.

```python
import math
import jax
import jax.numpy as jnp
from jax import lax

HEADS = 80
HEAD_DIM = 64
STATE = 128
SPAN = 256
SEG = 8
NDOC = 6
TOK_DEV = 1280
BINS = 32
LEN = 5120
ROWS = 163840
CAP = 48
WIDTH = 5120


def sudden_rows(key):
    hits = jax.random.randint(jax.random.fold_in(key, 11), (ROWS, 1), 0, max(LEN // 2, 2))
    return hits == 0


def draw_step_rows(key, part):
    offset_key = jax.random.fold_in(key, 21)
    rough_key = jax.random.fold_in(key, 22)
    start_offsets = jax.random.uniform(offset_key, (ROWS // TOK_DEV, 1), jnp.float32, -1.0, 1.0)
    start_offsets = jnp.repeat(start_offsets, TOK_DEV, axis=0)
    jitter_level = jnp.clip(jax.random.normal(rough_key, (ROWS, HEADS), jnp.float32), -4.0, 4.0)
    unscaled_steps = jnp.where(sudden_rows(key), 1000.0, -1.0 + start_offsets + jitter_level)
    return unscaled_steps.astype(jnp.bfloat16)


def draw_key_rows(key, part):
    base_key = jax.random.fold_in(key, 23)
    table_items = jnp.clip(0.3 * jax.random.normal(base_key, (ROWS, STATE), jnp.float32), -1.8, 1.8)
    table_items = jnp.where(sudden_rows(key), 0.002 * table_items, table_items)
    return table_items.astype(jnp.bfloat16)


def draw_decay_log(key, part):
    ranking = jax.random.permutation(jax.random.fold_in(key, 31), HEADS)
    slow_count = HEADS // 2
    slow_heads = ranking < slow_count
    spread = jax.random.uniform(jax.random.fold_in(key, 32), (HEADS,), jnp.float32, 0.0, 1.0)
    slow_log = math.log(0.0001) + spread * math.log(4.0)
    fast_log = math.log(0.05) + spread * math.log(3.0)
    return jnp.where(slow_heads, slow_log, fast_log).astype(jnp.float32)


def shuffle_segments(subkey):
    return jax.random.permutation(subkey, TOK_DEV // SEG)


def draw_source_rows(key, part):
    shard_number = LEN // TOK_DEV
    segment_count = TOK_DEV // SEG
    most_segments = CAP // SEG
    columns = []
    for column in range(shard_number):
        column_key = jax.random.fold_in(key, 100 + column)
        subkeys = jax.random.split(column_key, 6)
        heavy = jax.random.randint(subkeys[0], (), 0, BINS)
        offset_start = jax.random.randint(subkeys[1], (), 0, BINS - 1)
        others = (heavy + 1 + (offset_start + jnp.arange(segment_count - most_segments)) % (BINS - 1)) % BINS
        shifts = jnp.concatenate([jnp.full((most_segments,), heavy), others])
        first_perm = jax.random.permutation(subkeys[2], BINS)
        second_perm = jax.random.permutation(subkeys[3], BINS)
        sources = first_perm[(second_perm[:, None] + shifts[None, :]) % BINS]
        source_order = jax.vmap(shuffle_segments)(jax.random.split(subkeys[4], BINS))
        slot_order = jax.vmap(shuffle_segments)(jax.random.split(subkeys[5], BINS))
        source_at = jnp.take_along_axis(sources, slot_order, axis=1)
        segment_at = source_order[source_at, slot_order]
        inside = jnp.arange(SEG)
        row_start = (source_at * shard_number + column) * TOK_DEV + segment_at * SEG
        placed = row_start[:, :, None] + inside[None, None, :]
        columns.append(placed.reshape(BINS, TOK_DEV))
    return jnp.concatenate(columns, axis=1).astype(jnp.int32)


def pick_starts(subkey):
    chosen = jax.random.permutation(subkey, LEN - 1)[:NDOC - 1] + 1
    return jnp.sort(jnp.concatenate([jnp.zeros((1,), jnp.int32), chosen.astype(jnp.int32)]))


def draw_document_starts(key, part):
    return jax.vmap(pick_starts)(jax.random.split(jax.random.fold_in(key, 41), BINS))


def shard_levels(own_key, dims, cuts, least, high):
    level, own = 1.0, jax.random.fold_in(own_key, 6)
    for dim, shards_of in cuts:
        heights = jnp.exp(jax.random.uniform(jax.random.fold_in(own, dim), (shards_of,), jnp.float32, least / len(cuts), high / len(cuts)))
        level = level * jnp.repeat(heights, dims[dim] // shards_of).reshape([-1 if axis == dim else 1 for axis in range(len(dims))])
    return level


def scatter_about(own_key, extent, scale, reach, cuts=(), held_as=jnp.bfloat16):
    values = scale * jax.random.normal(own_key, extent, jnp.float32)
    if cuts:
        values = values * shard_levels(own_key, extent, cuts, -0.22, 0.18)
    return jnp.clip(values, -reach, reach).astype(held_as)


def setup_inputs(seed: int = 0) -> dict:
    splits = jax.random.split(jax.random.key(seed), 9)
    token_rows = scatter_about(splits[0], (ROWS, WIDTH), 1.0, 6.0, ((0, 128),))
    key_rows = draw_key_rows(jax.random.fold_in(splits[8], 71), 0)
    query_rows = scatter_about(splits[2], (ROWS, STATE), 0.03, 0.1796875, ((0, 128),))
    step_rows = draw_step_rows(jax.random.fold_in(splits[8], 71), 0)
    decay_log = draw_decay_log(jax.random.fold_in(splits[8], 71), 0)
    skip_gain = jnp.clip(jax.random.uniform(splits[5], (HEADS,), jnp.float32, 0.5, 1.5), 0.5, 1.5)
    source_rows = draw_source_rows(jax.random.fold_in(splits[8], 71), 0)
    document_starts = draw_document_starts(jax.random.fold_in(splits[8], 71), 0)
    return dict(token_rows=token_rows, key_rows=key_rows, query_rows=query_rows, step_rows=step_rows, decay_log=decay_log, skip_gain=skip_gain, source_rows=source_rows, document_starts=document_starts)


def span_pass(carried, pieces, decay_rate, skip_gain):
    values, keys_span, query_span, unscaled_steps, restart = pieces
    step_sizes = jax.nn.softplus(unscaled_steps.astype(jnp.float32))
    log_decay = -step_sizes * decay_rate[None, :]
    running_total = jnp.cumsum(log_decay, axis=0)
    document = jnp.cumsum(restart.astype(jnp.int32))
    position = jnp.arange(values.shape[0])
    linked = (document[:, None] == document[None, :]) & (position[None, :] <= position[:, None])
    scores = jnp.dot(query_span, keys_span.T, preferred_element_type=jnp.float32)
    decay_gap = running_total.T[:, :, None] - running_total.T[:, None, :]
    masked_gap = jnp.where(linked[None], decay_gap, -jnp.inf)
    weights = (scores[None] * jnp.exp(masked_gap) * step_sizes.T[:, None, :]).astype(jnp.bfloat16)
    within = jnp.einsum("hts,shp->thp", weights.astype(jnp.float32), values.astype(jnp.float32))
    entry_decay = jnp.where((document == 0)[:, None], jnp.exp(running_total), 0.0)
    from_state = jnp.einsum("tn,hnp->thp", query_span.astype(jnp.float32), carried,
                            precision=lax.Precision.HIGHEST) * entry_decay[:, :, None]
    to_end = running_total[-1][None, :] - running_total
    end_weight = jnp.where((document == document[-1])[:, None], jnp.exp(to_end), 0.0) * step_sizes
    scaled_values = (values.astype(jnp.float32) * end_weight[:, :, None]).astype(jnp.bfloat16)
    added_state = jnp.einsum("sn,shp->hnp", keys_span.astype(jnp.float32), scaled_values.astype(jnp.float32))
    retained = jnp.where(document[-1] == 0, jnp.exp(running_total[-1]), 0.0)
    carried = retained[:, None, None] * carried + added_state
    result = within + from_state + skip_gain[None, :, None] * values.astype(jnp.float32)
    return carried, result.astype(jnp.bfloat16)


def reference(token_rows, key_rows, query_rows, step_rows, decay_log, skip_gain, source_rows, document_starts):
    decay_rate = jnp.exp(decay_log)
    span_count = LEN // SPAN

    def advance(carried, pieces):
        return span_pass(carried, pieces, decay_rate, skip_gain)

    def one_sequence(inputs):
        wanted, starts = inputs
        values = jnp.take(token_rows, wanted, axis=0).reshape(span_count, SPAN, HEADS, HEAD_DIM)
        keys_packed = jnp.take(key_rows, wanted, axis=0).reshape(span_count, SPAN, STATE)
        query_packed = jnp.take(query_rows, wanted, axis=0).reshape(span_count, SPAN, STATE)
        steps_packed = jnp.take(step_rows, wanted, axis=0).reshape(span_count, SPAN, HEADS)
        position = jnp.arange(LEN)
        restart = jnp.any(position[:, None] == starts[None, :], axis=1).reshape(span_count, SPAN)
        zero_state = jnp.zeros((HEADS, STATE, HEAD_DIM), jnp.float32)
        final_state, results = lax.scan(advance, zero_state,
                                        (values, keys_packed, query_packed, steps_packed, restart))
        return results.reshape(LEN, HEADS * HEAD_DIM)

    return lax.map(one_sequence, (source_rows, document_starts))
```

```python
import functools
import math

import jax
import jax.numpy as jnp
from jax import lax
from jax.experimental import pallas as pl
from jax.experimental.pallas import tpu as pltpu
from jax.sharding import PartitionSpec as P

SPAN = 256
SEG = 8
LANES = 128
AUX = 3 * LANES
GROUP = 16
LOG2E = math.log2(math.e)
CEILING = 64.0

f32 = jnp.float32
bf16 = jnp.bfloat16


def params(mib, *semantics):
    return pltpu.CompilerParams(vmem_limit_bytes=mib * 2**20, dimension_semantics=semantics or None)


def estimate(flops, moved, exps=0):
    return pl.CostEstimate(flops=int(flops), bytes_accessed=int(moved), transcendentals=int(exps))


def pick_runs(ids, source, first, width, extra=None):
    count = ids.shape[0]
    more = 0 if extra is None else extra.shape[2]
    sources = (source,) if extra is None else (source, extra)

    def kernel(ids_ref, *refs):
        out_ref, sem = refs[-2:]

        @pl.loop(0, count)
        def _(i):
            run = ids_ref[i]
            pltpu.make_async_copy(
                refs[0].at[run, :, pl.ds(first, width)], out_ref.at[i, :, pl.ds(0, width)], sem
            ).start()
            if more:
                pltpu.make_async_copy(
                    refs[1].at[run], out_ref.at[i, :, pl.ds(width, more)], sem
                ).start()

        pltpu.make_async_copy(out_ref, out_ref, sem).wait()

    total = width + more
    return pl.pallas_call(
        kernel,
        out_shape=jax.ShapeDtypeStruct((count, SEG, total), source.dtype),
        grid_spec=pltpu.PrefetchScalarGridSpec(
            num_scalar_prefetch=1,
            grid=(1,),
            in_specs=[pl.BlockSpec(memory_space=pl.ANY)] * len(sources),
            out_specs=pl.BlockSpec(memory_space=pl.ANY),
            scratch_shapes=[pltpu.SemaphoreType.DMA],
        ),
        cost_estimate=estimate(0, 4 * count * SEG * total),
    )(ids, *sources)


def side_rows(key_rows, query_rows, step_rows):
    tokens, heads = step_rows.shape

    def kernel(k_ref, q_ref, st_ref, out_ref):
        out_ref[:, 0:LANES] = k_ref[...]
        out_ref[:, LANES : 2 * LANES] = q_ref[...]
        steps = st_ref[...].astype(f32)
        steps = jnp.concatenate([steps, jnp.zeros((LANES - heads, tokens), f32)], axis=0)
        out_ref[:, 2 * LANES : AUX] = jnp.transpose(steps).astype(bf16)

    return pl.pallas_call(
        kernel,
        out_shape=jax.ShapeDtypeStruct((tokens, AUX), bf16),
        compiler_params=params(32),
        cost_estimate=estimate(0, 4 * tokens * AUX),
    )(key_rows, query_rows, step_rows.T)


def prepare(packed, columns, decay_row, scalars):
    tokens = packed.shape[0]
    spans = tokens // SPAN
    starts = scalars.shape[0] - 1

    def kernel(
        sc_ref, k_ref, q_ref, st_ref, dec_ref,
        cum_ref, rt_ref, score_ref, kt_ref, endw_ref, entry_ref, entd_ref, ret_ref, thru_ref, pref,
    ):
        j = pl.program_id(0)

        @pl.when(j == 0)
        def _():
            pref[...] = jnp.ones_like(pref)

        raw = st_ref[...].astype(f32)
        step = jnp.maximum(raw, 0.0) + jnp.log1p(jnp.exp(-jnp.abs(raw)))
        decay = step * (jnp.exp(dec_ref[...]) * (-LOG2E))
        row = lax.broadcasted_iota(jnp.int32, (SPAN, SPAN), 0)
        col = lax.broadcasted_iota(jnp.int32, (SPAN, SPAN), 1)
        tri = (col <= row).astype(f32)
        cum = jnp.dot(tri, decay, precision=lax.Precision.HIGHEST, preferred_element_type=f32)
        begin = sc_ref[starts] + j * SPAN
        doc_row = jnp.zeros((SPAN, SPAN), jnp.int32)
        doc_col = jnp.zeros((SPAN, SPAN), jnp.int32)
        doc_tok = jnp.zeros((SPAN, LANES), jnp.int32)
        token = lax.broadcasted_iota(jnp.int32, (SPAN, LANES), 0)
        doc_end = jnp.int32(0)
        for d in range(starts):
            at = sc_ref[d] - begin
            at = jnp.where(at < 0, SPAN, at)
            doc_row += (at <= row).astype(jnp.int32)
            doc_col += (at <= col).astype(jnp.int32)
            doc_tok += (at <= token).astype(jnp.int32)
            doc_end += (at < SPAN).astype(jnp.int32)
        linked = (doc_row == doc_col) & (col <= row)
        scores = lax.dot_general(
            q_ref[...], k_ref[...], (((1,), (1,)), ((), ())), preferred_element_type=f32
        )
        score_ref[0] = jnp.where(linked, scores, 0.0)
        last = cum[SPAN - 1 : SPAN, :]
        cum_ref[...] = cum
        rt_ref[0] = jnp.transpose(cum - jnp.log(step) * LOG2E)
        kt_ref[0] = jnp.transpose(k_ref[...].astype(f32)).astype(bf16)
        endw_ref[...] = jnp.where(doc_tok == doc_end, jnp.exp2(last - cum), 0.0) * step
        entry = jnp.where(doc_tok == 0, jnp.exp2(cum), 0.0)
        entry_ref[...] = entry
        entd_ref[...] = entry * pref[0:1, :]
        kept = jnp.where(doc_end == 0, jnp.exp2(last), 0.0)
        kept = jnp.broadcast_to(kept, (8, LANES))
        ret_ref[0] = kept
        pref[...] = pref[...] * kept
        thru_ref[...] = pref[...]

    block = columns // LANES
    span_rows = pl.BlockSpec((SPAN, LANES), lambda j, s: (j, 0))
    rows = jax.ShapeDtypeStruct((tokens, LANES), f32)
    return pl.pallas_call(
        kernel,
        out_shape=(
            rows,
            jax.ShapeDtypeStruct((spans, LANES, SPAN), f32),
            jax.ShapeDtypeStruct((spans, SPAN, SPAN), f32),
            jax.ShapeDtypeStruct((spans, LANES, SPAN), bf16),
            rows,
            rows,
            rows,
            jax.ShapeDtypeStruct((spans, 8, LANES), f32),
            jax.ShapeDtypeStruct((8, LANES), f32),
        ),
        grid_spec=pltpu.PrefetchScalarGridSpec(
            num_scalar_prefetch=1,
            grid=(spans,),
            in_specs=[
                pl.BlockSpec((SPAN, LANES), lambda j, s: (j, block)),
                pl.BlockSpec((SPAN, LANES), lambda j, s: (j, block + 1)),
                pl.BlockSpec((SPAN, LANES), lambda j, s: (j, block + 2)),
                pl.BlockSpec((1, LANES), lambda j, s: (0, 0)),
            ],
            out_specs=[
                span_rows,
                pl.BlockSpec((1, LANES, SPAN), lambda j, s: (j, 0, 0)),
                pl.BlockSpec((1, SPAN, SPAN), lambda j, s: (j, 0, 0)),
                pl.BlockSpec((1, LANES, SPAN), lambda j, s: (j, 0, 0)),
                span_rows,
                span_rows,
                span_rows,
                pl.BlockSpec((1, 8, LANES), lambda j, s: (j, 0, 0)),
                pl.BlockSpec((8, LANES), lambda j, s: (0, 0)),
            ],
            scratch_shapes=[pltpu.VMEM((8, LANES), f32)],
        ),
        compiler_params=params(32, "arbitrary"),
        cost_estimate=estimate(spans * 2 * SPAN * SPAN * LANES * 7, 6 * 2**20),
    )(scalars, packed, packed, packed, decay_row)


def roll_heads(table, first_head):
    return pltpu.roll(table, lax.rem(LANES - first_head, LANES), 1)


def spreader(width, head_width):
    lane = lax.broadcasted_iota(jnp.int32, (2 * LANES, width), 1) // head_width
    source = lax.rem(lax.broadcasted_iota(jnp.int32, (2 * LANES, width), 0), LANES)
    return (lane == source).astype(bf16)


def halves(x):
    high = x.astype(bf16)
    return high, (x - high.astype(f32)).astype(bf16)


def spread(table, matrix):
    return jnp.dot(jnp.concatenate(halves(table), axis=1), matrix, preferred_element_type=f32)


def states(packed, width, first_head, head_width, kt, endw, ret, thru):
    tokens = packed.shape[0]
    spans = tokens // SPAN
    step_width = GROUP * head_width
    groups = width // step_width

    def kernel(v_ref, kt_ref, endw_ref, ret_ref, thru_ref, final_ref, enter_ref, state, matrix):
        g, j = pl.program_id(0), pl.program_id(1)
        head = first_head + g * GROUP

        @pl.when((g == 0) & (j == 0))
        def _():
            matrix[...] = spreader(step_width, head_width)

        @pl.when(j == 0)
        def _():
            state[...] = jnp.zeros_like(state)

        repeat = matrix[...]
        weight = spread(roll_heads(endw_ref[...], head), repeat)
        scaled = (v_ref[...].astype(f32) * weight).astype(bf16)
        added = jnp.dot(kt_ref[0], scaled, preferred_element_type=f32)
        kept = spread(roll_heads(ret_ref[0], head), repeat)[0:1, :]
        old = state[...]
        high, low = halves(old)
        enter_ref[0, 0:LANES, :] = high
        enter_ref[0, LANES : 2 * LANES, :] = low
        new = kept * old + added
        state[...] = new
        final_ref[0:LANES, :] = new.astype(bf16)
        through = spread(roll_heads(thru_ref[...], head), repeat)
        high, low = halves(through)
        final_ref[LANES : LANES + 16, :] = jnp.concatenate([high, low], axis=0)

    return pl.pallas_call(
        kernel,
        out_shape=(
            jax.ShapeDtypeStruct((LANES + 16, width), bf16),
            jax.ShapeDtypeStruct((spans, 2 * LANES, width), bf16),
        ),
        grid=(groups, spans),
        in_specs=[
            pl.BlockSpec((SPAN, step_width), lambda g, j: (j, g)),
            pl.BlockSpec((1, LANES, SPAN), lambda g, j: (j, 0, 0)),
            pl.BlockSpec((SPAN, LANES), lambda g, j: (j, 0)),
            pl.BlockSpec((1, 8, LANES), lambda g, j: (j, 0, 0)),
            pl.BlockSpec((8, LANES), lambda g, j: (0, 0)),
        ],
        out_specs=[
            pl.BlockSpec((LANES + 16, step_width), lambda g, j: (0, g)),
            pl.BlockSpec((1, 2 * LANES, step_width), lambda g, j: (j, 0, g)),
        ],
        scratch_shapes=[
            pltpu.VMEM((LANES, step_width), f32),
            pltpu.VMEM((2 * LANES, step_width), bf16),
        ],
        compiler_params=params(32, "arbitrary", "arbitrary"),
        cost_estimate=estimate(2 * tokens * width * 2.5 * LANES, 5 * tokens * width),
    )(packed, kt, endw, ret, thru)


def local_results(
    packed, width, first_head, head_width, whole_width, query_at, aux, cum, rt, scores, entry, enter, skip_row, result
):
    tokens = packed.shape[0]
    spans = tokens // SPAN
    step_width = GROUP * head_width
    groups = width // step_width
    first_group = first_head // GROUP
    half = SPAN // 2

    def kernel(v_ref, q_ref, cum_ref, rt_ref, score_ref, entry_ref, enter_ref, skip_ref, *rest):
        out_ref, matrix = rest[-2:]
        j, g = pl.program_id(0), pl.program_id(1)
        head = first_head + g * GROUP

        @pl.when((g == 0) & (j == 0))
        def _():
            matrix[...] = spreader(step_width, head_width)

        query = q_ref[...]
        base = jnp.dot(
            jnp.concatenate([query, query], axis=1), enter_ref[0], preferred_element_type=f32
        )
        base = base * spread(roll_heads(entry_ref[...], head), matrix[...])
        base = base + skip_ref[...] * v_ref[...].astype(f32)
        total = roll_heads(cum_ref[...], head)
        lane = lax.broadcasted_iota(jnp.int32, (half, 2 * head_width), 1)
        first_row = pl.multiple_of(head, 8)
        for pair in range(GROUP // 2):
            at = pair * 2 * head_width
            values = v_ref[:, at : at + 2 * head_width]
            for part in range(2):
                reach = (part + 1) * half
                rows = slice(part * half, reach)
                outs = []
                for h in (2 * pair, 2 * pair + 1):
                    from_row = rt_ref[0, pl.ds(first_row + 8 * (h // 8), 8), 0:reach][h % 8 : h % 8 + 1, :]
                    gap = total[rows, h : h + 1] - from_row
                    weights = score_ref[0, rows, 0:reach] * jnp.exp2(jnp.minimum(gap, CEILING))
                    outs.append(
                        jnp.dot(weights.astype(bf16), values[0:reach], preferred_element_type=f32)
                    )
                within = jnp.where(lane < head_width, outs[0], outs[1])
                out_ref[rows, at : at + 2 * head_width] = (
                    within + base[rows, at : at + 2 * head_width]
                ).astype(out_ref.dtype)

    rows = pl.BlockSpec((SPAN, LANES), lambda j, g: (j, 0))
    earlier = [] if result is None else [result]
    return pl.pallas_call(
        kernel,
        out_shape=jax.ShapeDtypeStruct((tokens, whole_width), bf16),
        grid=(spans, groups),
        in_specs=[
            pl.BlockSpec((SPAN, step_width), lambda j, g: (j, g)),
            pl.BlockSpec((SPAN, LANES), lambda j, g: (j, query_at)),
            rows,
            pl.BlockSpec((1, LANES, SPAN), lambda j, g: (j, 0, 0)),
            pl.BlockSpec((1, SPAN, SPAN), lambda j, g: (j, 0, 0)),
            rows,
            pl.BlockSpec((1, 2 * LANES, step_width), lambda j, g: (j, 0, g)),
            pl.BlockSpec((1, step_width), lambda j, g: (0, first_group + g)),
        ]
        + [pl.BlockSpec(memory_space=pl.ANY)] * len(earlier),
        out_specs=pl.BlockSpec((SPAN, step_width), lambda j, g: (j, first_group + g)),
        scratch_shapes=[pltpu.VMEM((2 * LANES, step_width), bf16)],
        input_output_aliases={8: 0} if earlier else {},
        compiler_params=params(48, "arbitrary", "arbitrary"),
        cost_estimate=estimate(
            2 * tokens * width * 4 * SPAN, 6 * tokens * width, tokens * SPAN * width // head_width
        ),
    )(packed, aux, cum, rt, scores, entry, enter, skip_row, *earlier)


def add_entering(result, width, first_head, head_width, query_at, aux, entd, arrived):
    tokens = result.shape[0]
    spans = tokens // SPAN
    step_width = GROUP * head_width
    groups = width // step_width
    first_group = first_head // GROUP

    def kernel(q_ref, entd_ref, *rest):
        froms = rest[: len(arrived)]
        in_ref, out_ref, matrix, state = rest[len(arrived) :]
        g, j = pl.program_id(0), pl.program_id(1)
        head = first_head + g * GROUP

        @pl.when((g == 0) & (j == 0))
        def _():
            matrix[...] = spreader(step_width, head_width)

        @pl.when(j == 0)
        def _():
            incoming = froms[-1][0:LANES, :].astype(f32)
            for ref in reversed(froms[:-1]):
                factor = ref[LANES : LANES + 16, :].astype(f32)
                incoming = ref[0:LANES, :].astype(f32) + (factor[0:1, :] + factor[8:9, :]) * incoming
            state[...] = incoming.astype(bf16)

        part = jnp.dot(q_ref[...], state[...], preferred_element_type=f32)
        part = part * spread(roll_heads(entd_ref[...], head), matrix[...])
        out_ref[...] = (in_ref[...].astype(f32) + part).astype(out_ref.dtype)

    place = pl.BlockSpec((SPAN, step_width), lambda g, j: (j, first_group + g))
    return pl.pallas_call(
        kernel,
        out_shape=jax.ShapeDtypeStruct(result.shape, result.dtype),
        grid=(groups, spans),
        in_specs=[
            pl.BlockSpec((SPAN, LANES), lambda g, j: (j, query_at)),
            pl.BlockSpec((SPAN, LANES), lambda g, j: (j, 0)),
        ]
        + [pl.BlockSpec((LANES + 16, step_width), lambda g, j: (0, g))] * len(arrived)
        + [place],
        out_specs=place,
        scratch_shapes=[
            pltpu.VMEM((2 * LANES, step_width), bf16),
            pltpu.VMEM((LANES, step_width), bf16),
        ],
        input_output_aliases={2 + len(arrived): 0},
        compiler_params=params(32, "arbitrary", "arbitrary"),
        cost_estimate=estimate(2 * tokens * width * 3 * LANES, 4 * tokens * width),
    )(aux, entd, *arrived, result)


def shifted(block, distance):
    count = lax.axis_size("seq")
    return lax.ppermute(block, "seq", [(i, i + distance) for i in range(count - distance)])


def on_device(
    token_rows, key_rows, query_rows, step_rows, decay_log, skip_gain, source_rows, document_starts
):
    tokens, whole_width = token_rows.shape
    peers = lax.axis_size("dp")
    shards = lax.axis_size("seq")
    heads = decay_log.shape[0]
    head_width = whole_width // heads
    runs = tokens // SEG
    capacity = runs // peers + 1

    first_rows = source_rows[0].reshape(runs, SEG)[:, 0]
    peer = first_rows // (tokens * shards)
    run = (first_rows % tokens) // SEG
    order = jnp.arange(runs)
    earlier = (peer[:, None] == peer[None, :]) & (order[None, :] < order[:, None])
    slot = peer * capacity + jnp.sum(earlier.astype(jnp.int32), axis=1)
    asked = jnp.sum(
        jnp.where(slot[None, :] == jnp.arange(peers * capacity)[:, None], run[None, :], 0), axis=1
    )
    wanted = lax.all_to_all(
        asked.reshape(peers, capacity), "dp", split_axis=0, concat_axis=0, tiled=True
    ).reshape(peers * capacity)

    aux_rows = side_rows(key_rows, query_rows, step_rows).reshape(runs, SEG, AUX)
    token_runs = token_rows.reshape(runs, SEG, whole_width)

    def exchange(block):
        rows = block.reshape(peers, capacity * SEG, block.shape[2])
        rows = lax.all_to_all(rows, "dp", split_axis=0, concat_axis=0, tiled=True)
        return rows.reshape(block.shape)

    last_width = GROUP * head_width
    main_width = whole_width - last_width
    main_heads = heads - GROUP
    sent_main = pick_runs(wanted, token_runs, 0, main_width, aux_rows)
    got_main = exchange(sent_main)
    wanted, sent_main = lax.optimization_barrier((wanted, sent_main))
    sent_last = pick_runs(wanted, token_runs, main_width, last_width)
    got_main, sent_last = lax.optimization_barrier((got_main, sent_last))
    got_last = exchange(sent_last)

    packed_main = pick_runs(slot, got_main, 0, main_width + AUX).reshape(tokens, main_width + AUX)
    scalars = jnp.concatenate(
        [document_starts[0], (lax.axis_index("seq") * tokens).astype(jnp.int32)[None]]
    )
    decay_row = jnp.pad(decay_log, (0, LANES - heads))[None, :]
    skip_row = jnp.repeat(skip_gain, head_width)[None, :]
    cum, rt, scores, kt, endw, entry, entd, ret, thru = prepare(
        packed_main, main_width, decay_row, scalars
    )
    query_at = main_width // LANES + 1
    distances = range(1, shards)

    final_main, enter_main = states(packed_main, main_width, 0, head_width, kt, endw, ret, thru)
    arrived_main = [shifted(final_main, d) for d in distances]
    packed_last = pick_runs(slot, got_last, 0, last_width).reshape(tokens, last_width)
    final_last, enter_last = states(
        packed_last, last_width, main_heads, head_width, kt, endw, ret, thru
    )
    arrived_last = [shifted(final_last, d) for d in distances]

    result = local_results(
        packed_main, main_width, 0, head_width, whole_width, query_at, packed_main, cum, rt, scores,
        entry, enter_main, skip_row, None,
    )
    result = local_results(
        packed_last, last_width, main_heads, head_width, whole_width, query_at, packed_main, cum, rt,
        scores, entry, enter_last, skip_row, result,
    )
    result = add_entering(
        result, main_width, 0, head_width, query_at, packed_main, entd, arrived_main
    )
    result = add_entering(
        result, last_width, main_heads, head_width, query_at, packed_main, entd, arrived_last
    )
    return result[None]


def solution(mesh):
    in_specs = (
        P(("dp", "seq"), None),
        P(("dp", "seq"), None),
        P(("dp", "seq"), None),
        P(("dp", "seq"), None),
        P(),
        P(),
        P("dp", "seq"),
        P("dp", None),
    )
    out_specs = P("dp", "seq", None)
    return jax.shard_map(
        on_device, mesh=mesh, in_specs=in_specs, out_specs=out_specs, check_vma=False
    )
```

```python
import functools
import math

import jax
import jax.numpy as jnp
from jax import lax
from jax.experimental import pallas as pl
from jax.experimental.pallas import tpu as pltpu
from jax.sharding import PartitionSpec as P

SPAN = 256
SEG = 8
LANES = 128
AUX = 3 * LANES
GROUP = 16
PARTS = (32, 32, 16)
CHUNK = 16
LOG2E = math.log2(math.e)
CEILING = 64.0

f32 = jnp.float32
bf16 = jnp.bfloat16


def params(mib, *semantics):
    return pltpu.CompilerParams(vmem_limit_bytes=mib * 2**20, dimension_semantics=semantics or None)


def estimate(flops, moved, exps=0):
    return pl.CostEstimate(flops=int(flops), bytes_accessed=int(moved), transcendentals=int(exps))


def pick_runs(ids, source, first, width, extra=None):
    count = ids.shape[0]
    more = 0 if extra is None else extra.shape[2]
    sources = (source,) if extra is None else (source, extra)
    total = width + more
    chunk = max(n for n in range(1, CHUNK + 1) if count % n == 0)
    chunks = count // chunk

    def kernel(ids_ref, *refs):
        out_ref, held, in_sems, out_sems = refs[-4:]

        @pl.loop(0, chunks)
        def _(c):
            @pl.loop(0, chunk)
            def _(i):
                place = c * chunk + i
                run = ids_ref[place]
                pltpu.make_async_copy(
                    refs[0].at[run, :, pl.ds(first, width)],
                    held.at[place, :, pl.ds(0, width)],
                    in_sems.at[c],
                ).start()
                if more:
                    pltpu.make_async_copy(
                        refs[1].at[run], held.at[place, :, pl.ds(width, more)], in_sems.at[c]
                    ).start()

        @pl.loop(0, chunks)
        def _(c):
            part = pl.ds(c * chunk, chunk)
            pltpu.make_async_copy(held.at[part], held.at[part], in_sems.at[c]).wait()
            pltpu.make_async_copy(held.at[part], out_ref.at[part], out_sems.at[c]).start()

        @pl.loop(0, chunks)
        def _(c):
            part = pl.ds(c * chunk, chunk)
            pltpu.make_async_copy(held.at[part], out_ref.at[part], out_sems.at[c]).wait()

    return pl.pallas_call(
        kernel,
        out_shape=jax.ShapeDtypeStruct((count, SEG, total), source.dtype),
        grid_spec=pltpu.PrefetchScalarGridSpec(
            num_scalar_prefetch=1,
            grid=(1,),
            in_specs=[pl.BlockSpec(memory_space=pl.ANY)] * len(sources),
            out_specs=pl.BlockSpec(memory_space=pl.ANY),
            scratch_shapes=[
                pltpu.VMEM((count, SEG, total), source.dtype),
                pltpu.SemaphoreType.DMA((chunks,)),
                pltpu.SemaphoreType.DMA((chunks,)),
            ],
        ),
        compiler_params=params(56),
        cost_estimate=estimate(0, 4 * count * SEG * total),
    )(ids, *sources)


def side_rows(key_rows, query_rows, step_rows):
    tokens, heads = step_rows.shape

    def kernel(k_ref, q_ref, st_ref, out_ref):
        out_ref[:, 0:LANES] = k_ref[...]
        out_ref[:, LANES : 2 * LANES] = q_ref[...]
        steps = st_ref[...].astype(f32)
        steps = jnp.concatenate([steps, jnp.zeros((LANES - heads, tokens), f32)], axis=0)
        out_ref[:, 2 * LANES : AUX] = jnp.transpose(steps).astype(bf16)

    return pl.pallas_call(
        kernel,
        out_shape=jax.ShapeDtypeStruct((tokens, AUX), bf16),
        compiler_params=params(32),
        cost_estimate=estimate(0, 4 * tokens * AUX),
    )(key_rows, query_rows, step_rows.T)


def prepare(packed, columns, decay_row, scalars):
    tokens = packed.shape[0]
    spans = tokens // SPAN
    starts = scalars.shape[0] - 1

    def kernel(
        sc_ref, k_ref, q_ref, st_ref, dec_ref,
        cum_ref, rt_ref, score_ref, kt_ref, endw_ref, entry_ref, entd_ref, ret_ref, thru_ref, pref,
    ):
        j = pl.program_id(0)

        @pl.when(j == 0)
        def _():
            pref[...] = jnp.ones_like(pref)

        raw = st_ref[...].astype(f32)
        step = jnp.maximum(raw, 0.0) + jnp.log1p(jnp.exp(-jnp.abs(raw)))
        decay = step * (jnp.exp(dec_ref[...]) * (-LOG2E))
        row = lax.broadcasted_iota(jnp.int32, (SPAN, SPAN), 0)
        col = lax.broadcasted_iota(jnp.int32, (SPAN, SPAN), 1)
        tri = (col <= row).astype(f32)
        cum = jnp.dot(tri, decay, precision=lax.Precision.HIGHEST, preferred_element_type=f32)
        begin = sc_ref[starts] + j * SPAN
        doc_row = jnp.zeros((SPAN, SPAN), jnp.int32)
        doc_col = jnp.zeros((SPAN, SPAN), jnp.int32)
        doc_tok = jnp.zeros((SPAN, LANES), jnp.int32)
        token = lax.broadcasted_iota(jnp.int32, (SPAN, LANES), 0)
        doc_end = jnp.int32(0)
        for d in range(starts):
            at = sc_ref[d] - begin
            at = jnp.where(at < 0, SPAN, at)
            doc_row += (at <= row).astype(jnp.int32)
            doc_col += (at <= col).astype(jnp.int32)
            doc_tok += (at <= token).astype(jnp.int32)
            doc_end += (at < SPAN).astype(jnp.int32)
        linked = (doc_row == doc_col) & (col <= row)
        scores = lax.dot_general(
            q_ref[...], k_ref[...], (((1,), (1,)), ((), ())), preferred_element_type=f32
        )
        score_ref[0] = jnp.where(linked, scores, 0.0)
        last = cum[SPAN - 1 : SPAN, :]
        cum_ref[...] = cum
        rt_ref[0] = jnp.transpose(cum - jnp.log(step) * LOG2E)
        kt_ref[0] = jnp.transpose(k_ref[...].astype(f32)).astype(bf16)
        endw_ref[...] = jnp.where(doc_tok == doc_end, jnp.exp2(last - cum), 0.0) * step
        entry = jnp.where(doc_tok == 0, jnp.exp2(cum), 0.0)
        entry_ref[...] = entry
        entd_ref[...] = entry * pref[0:1, :]
        kept = jnp.where(doc_end == 0, jnp.exp2(last), 0.0)
        kept = jnp.broadcast_to(kept, (8, LANES))
        ret_ref[0] = kept
        pref[...] = pref[...] * kept
        thru_ref[...] = pref[...]

    block = columns // LANES
    span_rows = pl.BlockSpec((SPAN, LANES), lambda j, s: (j, 0))
    rows = jax.ShapeDtypeStruct((tokens, LANES), f32)
    return pl.pallas_call(
        kernel,
        out_shape=(
            rows,
            jax.ShapeDtypeStruct((spans, LANES, SPAN), f32),
            jax.ShapeDtypeStruct((spans, SPAN, SPAN), f32),
            jax.ShapeDtypeStruct((spans, LANES, SPAN), bf16),
            rows,
            rows,
            rows,
            jax.ShapeDtypeStruct((spans, 8, LANES), f32),
            jax.ShapeDtypeStruct((8, LANES), f32),
        ),
        grid_spec=pltpu.PrefetchScalarGridSpec(
            num_scalar_prefetch=1,
            grid=(spans,),
            in_specs=[
                pl.BlockSpec((SPAN, LANES), lambda j, s: (j, block)),
                pl.BlockSpec((SPAN, LANES), lambda j, s: (j, block + 1)),
                pl.BlockSpec((SPAN, LANES), lambda j, s: (j, block + 2)),
                pl.BlockSpec((1, LANES), lambda j, s: (0, 0)),
            ],
            out_specs=[
                span_rows,
                pl.BlockSpec((1, LANES, SPAN), lambda j, s: (j, 0, 0)),
                pl.BlockSpec((1, SPAN, SPAN), lambda j, s: (j, 0, 0)),
                pl.BlockSpec((1, LANES, SPAN), lambda j, s: (j, 0, 0)),
                span_rows,
                span_rows,
                span_rows,
                pl.BlockSpec((1, 8, LANES), lambda j, s: (j, 0, 0)),
                pl.BlockSpec((8, LANES), lambda j, s: (0, 0)),
            ],
            scratch_shapes=[pltpu.VMEM((8, LANES), f32)],
        ),
        compiler_params=params(56, "arbitrary"),
        cost_estimate=estimate(spans * 2 * SPAN * SPAN * LANES * 7, 6 * 2**20),
    )(scalars, packed, packed, packed, decay_row)


def roll_heads(table, first_head):
    return pltpu.roll(table, lax.rem(LANES - first_head, LANES), 1)


def spreader(width, head_width):
    lane = lax.broadcasted_iota(jnp.int32, (2 * LANES, width), 1) // head_width
    source = lax.rem(lax.broadcasted_iota(jnp.int32, (2 * LANES, width), 0), LANES)
    return (lane == source).astype(bf16)


def halves(x):
    high = x.astype(bf16)
    return high, (x - high.astype(f32)).astype(bf16)


def spread(table, matrix):
    return jnp.dot(jnp.concatenate(halves(table), axis=1), matrix, preferred_element_type=f32)


def states(packed, width, first_head, head_width, kt, endw, ret, thru):
    tokens = packed.shape[0]
    spans = tokens // SPAN
    step_width = GROUP * head_width
    groups = width // step_width

    def kernel(v_ref, kt_ref, endw_ref, ret_ref, thru_ref, final_ref, enter_ref, state, matrix):
        g, j = pl.program_id(0), pl.program_id(1)
        head = first_head + g * GROUP

        @pl.when((g == 0) & (j == 0))
        def _():
            matrix[...] = spreader(step_width, head_width)

        @pl.when(j == 0)
        def _():
            state[...] = jnp.zeros_like(state)

        repeat = matrix[...]
        weight = spread(roll_heads(endw_ref[...], head), repeat)
        scaled = (v_ref[...].astype(f32) * weight).astype(bf16)
        added = jnp.dot(kt_ref[0], scaled, preferred_element_type=f32)
        kept = spread(roll_heads(ret_ref[0], head), repeat)[0:1, :]
        old = state[...]
        high, low = halves(old)
        enter_ref[0, 0:LANES, :] = high
        enter_ref[0, LANES : 2 * LANES, :] = low
        new = kept * old + added
        state[...] = new
        final_ref[0:LANES, :] = new.astype(bf16)
        through = spread(roll_heads(thru_ref[...], head), repeat)
        high, low = halves(through)
        final_ref[LANES : LANES + 16, :] = jnp.concatenate([high, low], axis=0)

    return pl.pallas_call(
        kernel,
        out_shape=(
            jax.ShapeDtypeStruct((LANES + 16, width), bf16),
            jax.ShapeDtypeStruct((spans, 2 * LANES, width), bf16),
        ),
        grid=(groups, spans),
        in_specs=[
            pl.BlockSpec((SPAN, step_width), lambda g, j: (j, g)),
            pl.BlockSpec((1, LANES, SPAN), lambda g, j: (j, 0, 0)),
            pl.BlockSpec((SPAN, LANES), lambda g, j: (j, 0)),
            pl.BlockSpec((1, 8, LANES), lambda g, j: (j, 0, 0)),
            pl.BlockSpec((8, LANES), lambda g, j: (0, 0)),
        ],
        out_specs=[
            pl.BlockSpec((LANES + 16, step_width), lambda g, j: (0, g)),
            pl.BlockSpec((1, 2 * LANES, step_width), lambda g, j: (j, 0, g)),
        ],
        scratch_shapes=[
            pltpu.VMEM((LANES, step_width), f32),
            pltpu.VMEM((2 * LANES, step_width), bf16),
        ],
        compiler_params=params(56, "arbitrary", "arbitrary"),
        cost_estimate=estimate(2 * tokens * width * 2.5 * LANES, 5 * tokens * width),
    )(packed, kt, endw, ret, thru)


def local_results(
    packed, width, first_head, head_width, whole_width, query_at, aux, cum, rt, scores, entry, enter, skip_row, result
):
    tokens = packed.shape[0]
    spans = tokens // SPAN
    step_width = GROUP * head_width
    groups = width // step_width
    first_group = first_head // GROUP
    half = SPAN // 2

    def kernel(v_ref, q_ref, cum_ref, rt_ref, score_ref, entry_ref, enter_ref, skip_ref, *rest):
        out_ref, matrix = rest[-2:]
        j, g = pl.program_id(0), pl.program_id(1)
        head = first_head + g * GROUP

        @pl.when((g == 0) & (j == 0))
        def _():
            matrix[...] = spreader(step_width, head_width)

        query = q_ref[...]
        base = jnp.dot(
            jnp.concatenate([query, query], axis=1), enter_ref[0], preferred_element_type=f32
        )
        base = base * spread(roll_heads(entry_ref[...], head), matrix[...])
        base = base + skip_ref[...] * v_ref[...].astype(f32)
        total = roll_heads(cum_ref[...], head)
        lane = lax.broadcasted_iota(jnp.int32, (half, 2 * head_width), 1)
        first_row = pl.multiple_of(head, 8)
        for pair in range(GROUP // 2):
            at = pair * 2 * head_width
            values = v_ref[:, at : at + 2 * head_width]
            for part in range(2):
                reach = (part + 1) * half
                rows = slice(part * half, reach)
                outs = []
                for h in (2 * pair, 2 * pair + 1):
                    from_row = rt_ref[0, pl.ds(first_row + 8 * (h // 8), 8), 0:reach][h % 8 : h % 8 + 1, :]
                    gap = total[rows, h : h + 1] - from_row
                    weights = score_ref[0, rows, 0:reach] * jnp.exp2(jnp.minimum(gap, CEILING))
                    outs.append(
                        jnp.dot(weights.astype(bf16), values[0:reach], preferred_element_type=f32)
                    )
                within = jnp.where(lane < head_width, outs[0], outs[1])
                out_ref[rows, at : at + 2 * head_width] = (
                    within + base[rows, at : at + 2 * head_width]
                ).astype(out_ref.dtype)

    rows = pl.BlockSpec((SPAN, LANES), lambda j, g: (j, 0))
    earlier = [] if result is None else [result]
    return pl.pallas_call(
        kernel,
        out_shape=jax.ShapeDtypeStruct((tokens, whole_width), bf16),
        grid=(spans, groups),
        in_specs=[
            pl.BlockSpec((SPAN, step_width), lambda j, g: (j, g)),
            pl.BlockSpec((SPAN, LANES), lambda j, g: (j, query_at)),
            rows,
            pl.BlockSpec((1, LANES, SPAN), lambda j, g: (j, 0, 0)),
            pl.BlockSpec((1, SPAN, SPAN), lambda j, g: (j, 0, 0)),
            rows,
            pl.BlockSpec((1, 2 * LANES, step_width), lambda j, g: (j, 0, g)),
            pl.BlockSpec((1, step_width), lambda j, g: (0, first_group + g)),
        ]
        + [pl.BlockSpec(memory_space=pl.ANY)] * len(earlier),
        out_specs=pl.BlockSpec((SPAN, step_width), lambda j, g: (j, first_group + g)),
        scratch_shapes=[pltpu.VMEM((2 * LANES, step_width), bf16)],
        input_output_aliases={8: 0} if earlier else {},
        compiler_params=params(56, "arbitrary", "arbitrary"),
        cost_estimate=estimate(
            2 * tokens * width * 4 * SPAN, 6 * tokens * width, tokens * SPAN * width // head_width
        ),
    )(packed, aux, cum, rt, scores, entry, enter, skip_row, *earlier)


def add_entering(result, width, first_head, head_width, query_at, aux, entd, arrived):
    tokens = result.shape[0]
    spans = tokens // SPAN
    step_width = GROUP * head_width
    groups = width // step_width
    first_group = first_head // GROUP

    def kernel(q_ref, entd_ref, *rest):
        froms = rest[: len(arrived)]
        in_ref, out_ref, matrix, state = rest[len(arrived) :]
        g, j = pl.program_id(0), pl.program_id(1)
        head = first_head + g * GROUP

        @pl.when((g == 0) & (j == 0))
        def _():
            matrix[...] = spreader(step_width, head_width)

        @pl.when(j == 0)
        def _():
            incoming = froms[-1][0:LANES, :].astype(f32)
            for ref in reversed(froms[:-1]):
                factor = ref[LANES : LANES + 16, :].astype(f32)
                incoming = ref[0:LANES, :].astype(f32) + (factor[0:1, :] + factor[8:9, :]) * incoming
            state[...] = incoming.astype(bf16)

        part = jnp.dot(q_ref[...], state[...], preferred_element_type=f32)
        part = part * spread(roll_heads(entd_ref[...], head), matrix[...])
        out_ref[...] = (in_ref[...].astype(f32) + part).astype(out_ref.dtype)

    place = pl.BlockSpec((SPAN, step_width), lambda g, j: (j, first_group + g))
    return pl.pallas_call(
        kernel,
        out_shape=jax.ShapeDtypeStruct(result.shape, result.dtype),
        grid=(groups, spans),
        in_specs=[
            pl.BlockSpec((SPAN, LANES), lambda g, j: (j, query_at)),
            pl.BlockSpec((SPAN, LANES), lambda g, j: (j, 0)),
        ]
        + [pl.BlockSpec((LANES + 16, step_width), lambda g, j: (0, g))] * len(arrived)
        + [place],
        out_specs=place,
        scratch_shapes=[
            pltpu.VMEM((2 * LANES, step_width), bf16),
            pltpu.VMEM((LANES, step_width), bf16),
        ],
        input_output_aliases={2 + len(arrived): 0},
        compiler_params=params(56, "arbitrary", "arbitrary"),
        cost_estimate=estimate(2 * tokens * width * 3 * LANES, 4 * tokens * width),
    )(aux, entd, *arrived, result)


def shifted(block, distance):
    count = lax.axis_size("seq")
    return lax.ppermute(block, "seq", [(i, i + distance) for i in range(count - distance)])


def on_device(
    token_rows, key_rows, query_rows, step_rows, decay_log, skip_gain, source_rows, document_starts
):
    tokens, whole_width = token_rows.shape
    peers = lax.axis_size("dp")
    shards = lax.axis_size("seq")
    heads = decay_log.shape[0]
    head_width = whole_width // heads
    runs = tokens // SEG
    capacity = runs // peers + 1

    first_rows = source_rows[0].reshape(runs, SEG)[:, 0]
    peer = first_rows // (tokens * shards)
    run = (first_rows % tokens) // SEG
    order = jnp.arange(runs)
    earlier = (peer[:, None] == peer[None, :]) & (order[None, :] < order[:, None])
    slot = peer * capacity + jnp.sum(earlier.astype(jnp.int32), axis=1)
    asked = jnp.sum(
        jnp.where(slot[None, :] == jnp.arange(peers * capacity)[:, None], run[None, :], 0), axis=1
    )
    wanted = lax.all_to_all(
        asked.reshape(peers, capacity), "dp", split_axis=0, concat_axis=0, tiled=True
    ).reshape(peers * capacity)

    aux_rows = side_rows(key_rows, query_rows, step_rows).reshape(runs, SEG, AUX)
    token_runs = token_rows.reshape(runs, SEG, whole_width)

    def exchange(block):
        rows = block.reshape(peers, capacity * SEG, block.shape[2])
        rows = lax.all_to_all(rows, "dp", split_axis=0, concat_axis=0, tiled=True)
        return rows.reshape(block.shape)

    widths = [n * head_width for n in PARTS]
    firsts = [sum(PARTS[:i]) for i in range(len(PARTS))]
    scalars = jnp.concatenate(
        [document_starts[0], (lax.axis_index("seq") * tokens).astype(jnp.int32)[None]]
    )
    decay_row = jnp.pad(decay_log, (0, LANES - heads))[None, :]
    skip_row = jnp.repeat(skip_gain, head_width)[None, :]
    query_at = widths[0] // LANES + 1
    parts = range(len(PARTS))

    sent = []
    for i in parts:
        sent.append(
            pick_runs(wanted, token_runs, firsts[i] * head_width, widths[i], None if i else aux_rows)
        )
        wanted, sent[i] = lax.optimization_barrier((wanted, sent[i]))
    got, packed, ends, arrived = [], [], [], []
    aux, tables, result = None, None, None

    def receive(i):
        nonlocal aux, tables
        columns = widths[i] if i else widths[i] + AUX
        packed.append(pick_runs(slot, got[i], 0, columns).reshape(tokens, columns))
        if not i:
            aux = packed[0]
            tables = prepare(aux, widths[0], decay_row, scalars)
        kt, endw, ret, thru = tables[3], tables[4], tables[7], tables[8]
        ends.append(states(packed[i], widths[i], firsts[i], head_width, kt, endw, ret, thru))
        arrived.append([shifted(ends[i][0], d) for d in range(1, shards)])

    def local(i, result):
        cum, rt, scores, entry = tables[0], tables[1], tables[2], tables[5]
        return local_results(
            packed[i], widths[i], firsts[i], head_width, whole_width, query_at, aux, cum, rt, scores,
            entry, ends[i][1], skip_row, result,
        )

    def entering(i, result):
        return add_entering(
            result, widths[i], firsts[i], head_width, query_at, aux, tables[6], arrived[i]
        )

    got.append(exchange(sent[0]))
    got[0], sent[1] = lax.optimization_barrier((got[0], sent[1]))
    got.append(exchange(sent[1]))
    receive(0)
    result = entering(0, local(0, result))
    got[1], sent[2], result = lax.optimization_barrier((got[1], sent[2], result))
    got.append(exchange(sent[2]))
    receive(1)
    result = local(1, result)
    receive(2)
    result = local(2, result)
    result = entering(1, result)
    result = entering(2, result)
    return result[None]


def solution(mesh):
    in_specs = (
        P(("dp", "seq"), None),
        P(("dp", "seq"), None),
        P(("dp", "seq"), None),
        P(("dp", "seq"), None),
        P(),
        P(),
        P("dp", "seq"),
        P("dp", None),
    )
    out_specs = P("dp", "seq", None)
    return jax.shard_map(
        on_device, mesh=mesh, in_specs=in_specs, out_specs=out_specs, check_vma=False
    )
```

```python
import functools
import math

import jax
import jax.numpy as jnp
from jax import lax
from jax.experimental import pallas as pl
from jax.experimental.pallas import tpu as pltpu
from jax.sharding import PartitionSpec as P

SPAN = 256
SEG = 8
LANES = 128
AUX = 3 * LANES
GROUP = 16
PARTS = (32, 32, 16)
CHUNK = 16
LOG2E = math.log2(math.e)
CEILING = 64.0

f32 = jnp.float32
bf16 = jnp.bfloat16


def params(mib, *semantics):
    return pltpu.CompilerParams(vmem_limit_bytes=mib * 2**20, dimension_semantics=semantics or None)


def estimate(flops, moved, exps=0):
    return pl.CostEstimate(flops=int(flops), bytes_accessed=int(moved), transcendentals=int(exps))


def pick_runs(ids, source, first, width, extra=None):
    count = ids.shape[0]
    more = 0 if extra is None else extra.shape[2]
    sources = (source,) if extra is None else (source, extra)
    total = width + more
    chunk = max(n for n in range(1, CHUNK + 1) if count % n == 0)
    chunks = count // chunk

    def kernel(ids_ref, *refs):
        out_ref, held, in_sems, out_sems = refs[-4:]

        @pl.loop(0, chunks)
        def _(c):
            @pl.loop(0, chunk)
            def _(i):
                place = c * chunk + i
                run = ids_ref[place]
                pltpu.make_async_copy(
                    refs[0].at[run, :, pl.ds(first, width)],
                    held.at[place, :, pl.ds(0, width)],
                    in_sems.at[c],
                ).start()
                if more:
                    pltpu.make_async_copy(
                        refs[1].at[run], held.at[place, :, pl.ds(width, more)], in_sems.at[c]
                    ).start()

        @pl.loop(0, chunks)
        def _(c):
            part = pl.ds(c * chunk, chunk)
            pltpu.make_async_copy(held.at[part], held.at[part], in_sems.at[c]).wait()
            pltpu.make_async_copy(held.at[part], out_ref.at[part], out_sems.at[c]).start()

        @pl.loop(0, chunks)
        def _(c):
            part = pl.ds(c * chunk, chunk)
            pltpu.make_async_copy(held.at[part], out_ref.at[part], out_sems.at[c]).wait()

    return pl.pallas_call(
        kernel,
        out_shape=jax.ShapeDtypeStruct((count, SEG, total), source.dtype),
        grid_spec=pltpu.PrefetchScalarGridSpec(
            num_scalar_prefetch=1,
            grid=(1,),
            in_specs=[pl.BlockSpec(memory_space=pl.ANY)] * len(sources),
            out_specs=pl.BlockSpec(memory_space=pl.ANY),
            scratch_shapes=[
                pltpu.VMEM((count, SEG, total), source.dtype),
                pltpu.SemaphoreType.DMA((chunks,)),
                pltpu.SemaphoreType.DMA((chunks,)),
            ],
        ),
        compiler_params=params(56),
        cost_estimate=estimate(0, 4 * count * SEG * total),
    )(ids, *sources)


def side_rows(key_rows, query_rows, step_rows):
    tokens, heads = step_rows.shape

    def kernel(k_ref, q_ref, st_ref, out_ref):
        out_ref[:, 0:LANES] = k_ref[...]
        out_ref[:, LANES : 2 * LANES] = q_ref[...]
        steps = st_ref[...].astype(f32)
        steps = jnp.concatenate([steps, jnp.zeros((LANES - heads, tokens), f32)], axis=0)
        out_ref[:, 2 * LANES : AUX] = jnp.transpose(steps).astype(bf16)

    return pl.pallas_call(
        kernel,
        out_shape=jax.ShapeDtypeStruct((tokens, AUX), bf16),
        compiler_params=params(32),
        cost_estimate=estimate(0, 4 * tokens * AUX),
    )(key_rows, query_rows, step_rows.T)


def prepare(packed, columns, decay_row, scalars):
    tokens = packed.shape[0]
    spans = tokens // SPAN
    starts = scalars.shape[0] - 1

    def kernel(
        sc_ref, k_ref, q_ref, st_ref, dec_ref,
        cum_ref, rt_ref, score_ref, kt_ref, endw_ref, entry_ref, entd_ref, ret_ref, thru_ref, pref,
    ):
        j = pl.program_id(0)

        @pl.when(j == 0)
        def _():
            pref[...] = jnp.ones_like(pref)

        raw = st_ref[...].astype(f32)
        step = jnp.maximum(raw, 0.0) + jnp.log1p(jnp.exp(-jnp.abs(raw)))
        decay = step * (jnp.exp(dec_ref[...]) * (-LOG2E))
        row = lax.broadcasted_iota(jnp.int32, (SPAN, SPAN), 0)
        col = lax.broadcasted_iota(jnp.int32, (SPAN, SPAN), 1)
        tri = (col <= row).astype(f32)
        cum = jnp.dot(tri, decay, precision=lax.Precision.HIGHEST, preferred_element_type=f32)
        begin = sc_ref[starts] + j * SPAN
        doc_row = jnp.zeros((SPAN, SPAN), jnp.int32)
        doc_col = jnp.zeros((SPAN, SPAN), jnp.int32)
        doc_tok = jnp.zeros((SPAN, LANES), jnp.int32)
        token = lax.broadcasted_iota(jnp.int32, (SPAN, LANES), 0)
        doc_end = jnp.int32(0)
        for d in range(starts):
            at = sc_ref[d] - begin
            at = jnp.where(at < 0, SPAN, at)
            doc_row += (at <= row).astype(jnp.int32)
            doc_col += (at <= col).astype(jnp.int32)
            doc_tok += (at <= token).astype(jnp.int32)
            doc_end += (at < SPAN).astype(jnp.int32)
        linked = (doc_row == doc_col) & (col <= row)
        scores = lax.dot_general(
            q_ref[...], k_ref[...], (((1,), (1,)), ((), ())), preferred_element_type=f32
        )
        score_ref[0] = jnp.where(linked, scores, 0.0)
        last = cum[SPAN - 1 : SPAN, :]
        cum_ref[...] = cum
        rt_ref[0] = jnp.transpose(cum - jnp.log(step) * LOG2E)
        kt_ref[0] = jnp.transpose(k_ref[...].astype(f32)).astype(bf16)
        endw_ref[...] = jnp.where(doc_tok == doc_end, jnp.exp2(last - cum), 0.0) * step
        entry = jnp.where(doc_tok == 0, jnp.exp2(cum), 0.0)
        entry_ref[...] = entry
        entd_ref[...] = entry * pref[0:1, :]
        kept = jnp.where(doc_end == 0, jnp.exp2(last), 0.0)
        kept = jnp.broadcast_to(kept, (8, LANES))
        ret_ref[0] = kept
        pref[...] = pref[...] * kept
        thru_ref[...] = pref[...]

    block = columns // LANES
    span_rows = pl.BlockSpec((SPAN, LANES), lambda j, s: (j, 0))
    rows = jax.ShapeDtypeStruct((tokens, LANES), f32)
    return pl.pallas_call(
        kernel,
        out_shape=(
            rows,
            jax.ShapeDtypeStruct((spans, LANES, SPAN), f32),
            jax.ShapeDtypeStruct((spans, SPAN, SPAN), f32),
            jax.ShapeDtypeStruct((spans, LANES, SPAN), bf16),
            rows,
            rows,
            rows,
            jax.ShapeDtypeStruct((spans, 8, LANES), f32),
            jax.ShapeDtypeStruct((8, LANES), f32),
        ),
        grid_spec=pltpu.PrefetchScalarGridSpec(
            num_scalar_prefetch=1,
            grid=(spans,),
            in_specs=[
                pl.BlockSpec((SPAN, LANES), lambda j, s: (j, block)),
                pl.BlockSpec((SPAN, LANES), lambda j, s: (j, block + 1)),
                pl.BlockSpec((SPAN, LANES), lambda j, s: (j, block + 2)),
                pl.BlockSpec((1, LANES), lambda j, s: (0, 0)),
            ],
            out_specs=[
                span_rows,
                pl.BlockSpec((1, LANES, SPAN), lambda j, s: (j, 0, 0)),
                pl.BlockSpec((1, SPAN, SPAN), lambda j, s: (j, 0, 0)),
                pl.BlockSpec((1, LANES, SPAN), lambda j, s: (j, 0, 0)),
                span_rows,
                span_rows,
                span_rows,
                pl.BlockSpec((1, 8, LANES), lambda j, s: (j, 0, 0)),
                pl.BlockSpec((8, LANES), lambda j, s: (0, 0)),
            ],
            scratch_shapes=[pltpu.VMEM((8, LANES), f32)],
        ),
        compiler_params=params(56, "arbitrary"),
        cost_estimate=estimate(spans * 2 * SPAN * SPAN * LANES * 7, 6 * 2**20),
    )(scalars, packed, packed, packed, decay_row)


def spreader(width, head_width, first_head):
    lane = lax.broadcasted_iota(jnp.int32, (LANES, width), 1)
    start = (lax.broadcasted_iota(jnp.int32, (LANES, width), 0) - first_head) * head_width
    once = ((lane >= start) & (lane < start + head_width)).astype(f32).astype(bf16)
    return jnp.concatenate([once, once], axis=0)


def halves(x):
    high = x.astype(bf16)
    return high, (x - high.astype(f32)).astype(bf16)


def summands(table):
    return jnp.concatenate(halves(table), axis=1)


def spread(pair, matrix):
    return jnp.dot(pair, matrix, preferred_element_type=f32)


def blocks(
    got, slot, width, first_head, head_width, tables, aux, query_at, skip_row, result, whole_width, with_end, with_local
):
    cum, rt, scores, kt, endw, entry, _, ret, thru = tables
    tokens = slot.shape[0] * SEG
    spans = tokens // SPAN
    step_width = GROUP * head_width
    groups = width // step_width
    place = first_head * head_width // width
    half = SPAN // 2
    runs = SPAN // SEG

    def kernel(slot_ref, *refs):
        refs = list(refs)
        got_ref, kt_ref, endw_ref, ret_ref, thru_ref = refs[:5]
        del refs[:5]
        if with_local:
            q_ref, cum_ref, rt_ref, score_ref, entry_ref, skip_ref = refs[:6]
            del refs[:6]
            if result is not None:
                del refs[:1]
        if with_end:
            final_ref = refs.pop(0)
        if with_local:
            out_ref = refs.pop(0)
            outs_held, out_sems = refs[-2:]
        state, matrix, held, sems = refs[:4]

        @pl.loop(0, spans)
        def _(j):
            @pl.loop(0, runs, unroll=8)
            def _(i):
                pltpu.make_async_copy(
                    got_ref.at[slot_ref[j * runs + i], :, pl.ds(0, width)], held.at[j, i], sems.at[j]
                ).start()

        state[...] = jnp.zeros_like(state)
        for g in range(groups):
            matrix[g] = spreader(step_width, head_width, first_head + g * GROUP)

        def written(j):
            return pltpu.make_async_copy(
                outs_held.at[lax.rem(j, 2)],
                out_ref.at[pl.ds(pl.multiple_of(j * SPAN, SPAN), SPAN), pl.ds(first_head * head_width, width)],
                out_sems.at[lax.rem(j, 2)],
            )

        @pl.loop(0, spans)
        def _(j):
            tokens_of = pl.ds(pl.multiple_of(j * SPAN, SPAN), SPAN)
            end_weight = summands(endw_ref[tokens_of, :])
            kept_all = summands(ret_ref[j])
            if with_local:
                entry_all = summands(entry_ref[tokens_of, :])
                query = q_ref[tokens_of, :]
                query = jnp.concatenate([query, query], axis=1)
                lane = lax.broadcasted_iota(jnp.int32, (half, 2 * head_width), 1)

                @pl.when(j >= 2)
                def _():
                    written(j - 2).wait()

            pltpu.make_async_copy(held.at[j], held.at[j], sems.at[j]).wait()

            for g in range(groups):
                head = first_head + g * GROUP
                columns = slice(g * step_width, (g + 1) * step_width)
                block = held[j, :, :, columns].reshape(SPAN, step_width)
                old = state[:, columns]
                scaled = block.astype(f32) * spread(end_weight, matrix[g])
                added = jnp.dot(kt_ref[j], scaled.astype(bf16), preferred_element_type=f32)
                state[:, columns] = spread(kept_all, matrix[g])[0:1, :] * old + added
                if not with_local:
                    continue
                base = jnp.dot(
                    query, jnp.concatenate(halves(old), axis=0), preferred_element_type=f32
                )
                base = base * spread(entry_all, matrix[g])
                base = base + skip_ref[:, columns] * block.astype(f32)
                for pair in range(GROUP // 2):
                    at = pair * 2 * head_width
                    values = block[:, at : at + 2 * head_width]
                    for part in range(2):
                        reach = (part + 1) * half
                        rows = slice(part * half, reach)
                        rows_of = pl.ds(pl.multiple_of(j * SPAN + part * half, half), half)
                        outs = []
                        for h in (head + 2 * pair, head + 2 * pair + 1):
                            gap = cum_ref[rows_of, h : h + 1] - rt_ref[j, h : h + 1, 0:reach]
                            weights = score_ref[j, rows, 0:reach] * jnp.exp2(
                                jnp.minimum(gap, CEILING)
                            )
                            outs.append(
                                jnp.dot(
                                    weights.astype(bf16), values[0:reach], preferred_element_type=f32
                                )
                            )
                        within = jnp.where(lane < head_width, outs[0], outs[1])
                        to = columns.start + at
                        outs_held[lax.rem(j, 2), rows, to : to + 2 * head_width] = (
                            within + base[rows, at : at + 2 * head_width]
                        ).astype(bf16)
            if with_local:
                written(j).start()

        if with_end:
            through_all = summands(thru_ref[...])
            for g in range(groups):
                columns = slice(g * step_width, (g + 1) * step_width)
                final_ref[0:LANES, columns] = state[:, columns].astype(bf16)
                high, low = halves(spread(through_all, matrix[g]))
                final_ref[LANES : LANES + 16, columns] = jnp.concatenate([high, low], axis=0)
        if with_local:
            for j in range(max(spans - 2, 0), spans):
                written(jnp.int32(j)).wait()

    def whole(array, columns=None, at=0):
        shape = array.shape if columns is None else array.shape[:-1] + (columns,)
        return pl.BlockSpec(shape, lambda i, s: (0,) * (len(shape) - 1) + (at,))

    anywhere = pl.BlockSpec(memory_space=pl.ANY)
    operands = [got, kt, endw, ret, thru]
    in_specs = [anywhere, whole(kt), whole(endw), whole(ret), whole(thru)]
    out_shape, out_specs, aliases = [], [], {}
    scratch = [
        pltpu.VMEM((LANES, width), f32),
        pltpu.VMEM((groups, 2 * LANES, step_width), bf16),
        pltpu.VMEM((spans, runs, SEG, width), bf16),
        pltpu.SemaphoreType.DMA((spans,)),
    ]
    if with_end:
        out_shape.append(jax.ShapeDtypeStruct((LANES + 16, width), bf16))
        out_specs.append(pl.BlockSpec((LANES + 16, width), lambda i, s: (0, 0)))
    if with_local:
        operands += [aux, cum, rt, scores, entry, skip_row]
        in_specs += [whole(aux, LANES, query_at), whole(cum), whole(rt), whole(scores), whole(entry)]
        in_specs.append(whole(skip_row, width, place))
        if result is not None:
            aliases = {1 + len(operands): len(out_shape)}
            operands.append(result)
            in_specs.append(anywhere)
        out_shape.append(jax.ShapeDtypeStruct((tokens, whole_width), bf16))
        out_specs.append(anywhere)
        scratch += [pltpu.VMEM((2, SPAN, width), bf16), pltpu.SemaphoreType.DMA((2,))]
    return pl.pallas_call(
        kernel,
        out_shape=tuple(out_shape),
        grid_spec=pltpu.PrefetchScalarGridSpec(
            num_scalar_prefetch=1,
            grid=(1,),
            in_specs=in_specs,
            out_specs=tuple(out_specs),
            scratch_shapes=scratch,
        ),
        input_output_aliases=aliases,
        compiler_params=params(56),
        cost_estimate=estimate(
            2 * tokens * width * (5 if with_local else 2) * SPAN,
            6 * tokens * width,
            tokens * SPAN * width // head_width if with_local else 0,
        ),
    )(slot, *operands)


def add_entering(result, width, first_head, head_width, query_at, aux, entd, arrived):
    tokens = result.shape[0]
    spans = tokens // SPAN
    step_width = GROUP * head_width
    groups = width // step_width

    def kernel(q_ref, entd_ref, *rest):
        froms = rest[: len(arrived)]
        in_ref, out_ref, matrix, state, held, in_sems, out_sems = rest[len(arrived) :]

        def place(ref, j):
            first = pl.multiple_of(j * SPAN, SPAN)
            return ref.at[pl.ds(first, SPAN), pl.ds(first_head * head_width, width)]

        @pl.loop(0, spans)
        def _(j):
            pltpu.make_async_copy(place(in_ref, j), held.at[j], in_sems.at[j]).start()

        for g in range(groups):
            matrix[g] = spreader(step_width, head_width, first_head + g * GROUP)
        incoming = froms[-1][0:LANES, :].astype(f32)
        for ref in reversed(froms[:-1]):
            factor = ref[LANES : LANES + 16, :].astype(f32)
            incoming = ref[0:LANES, :].astype(f32) + (factor[0:1, :] + factor[8:9, :]) * incoming
        state[...] = incoming.astype(bf16)

        @pl.loop(0, spans)
        def _(j):
            tokens_of = pl.ds(pl.multiple_of(j * SPAN, SPAN), SPAN)
            entry_all = summands(entd_ref[tokens_of, :])
            pltpu.make_async_copy(place(in_ref, j), held.at[j], in_sems.at[j]).wait()
            for g in range(groups):
                columns = slice(g * step_width, (g + 1) * step_width)
                part = jnp.dot(
                    q_ref[tokens_of, :], state[:, columns], preferred_element_type=f32
                )
                part = part * spread(entry_all, matrix[g])
                held[j, :, columns] = (held[j, :, columns].astype(f32) + part).astype(bf16)
            pltpu.make_async_copy(held.at[j], place(out_ref, j), out_sems.at[j]).start()

        @pl.loop(0, spans)
        def _(j):
            pltpu.make_async_copy(held.at[j], place(out_ref, j), out_sems.at[j]).wait()

    return pl.pallas_call(
        kernel,
        out_shape=jax.ShapeDtypeStruct(result.shape, result.dtype),
        grid=(1,),
        in_specs=[
            pl.BlockSpec((tokens, LANES), lambda i: (0, query_at)),
            pl.BlockSpec((tokens, LANES), lambda i: (0, 0)),
        ]
        + [pl.BlockSpec((LANES + 16, width), lambda i: (0, 0))] * len(arrived)
        + [pl.BlockSpec(memory_space=pl.ANY)],
        out_specs=pl.BlockSpec(memory_space=pl.ANY),
        scratch_shapes=[
            pltpu.VMEM((groups, 2 * LANES, step_width), bf16),
            pltpu.VMEM((LANES, width), bf16),
            pltpu.VMEM((spans, SPAN, width), bf16),
            pltpu.SemaphoreType.DMA((spans,)),
            pltpu.SemaphoreType.DMA((spans,)),
        ],
        input_output_aliases={2 + len(arrived): 0},
        compiler_params=params(56),
        cost_estimate=estimate(2 * tokens * width * 3 * LANES, 4 * tokens * width),
    )(aux, entd, *arrived, result)


def shifted(block, distance):
    count = lax.axis_size("seq")
    return lax.ppermute(block, "seq", [(i, i + distance) for i in range(count - distance)])


def on_device(
    token_rows, key_rows, query_rows, step_rows, decay_log, skip_gain, source_rows, document_starts
):
    tokens, whole_width = token_rows.shape
    peers = lax.axis_size("dp")
    shards = lax.axis_size("seq")
    heads = decay_log.shape[0]
    head_width = whole_width // heads
    runs = tokens // SEG
    capacity = runs // peers + 1

    first_rows = source_rows[0].reshape(runs, SEG)[:, 0]
    peer = first_rows // (tokens * shards)
    run = (first_rows % tokens) // SEG
    order = jnp.arange(runs)
    earlier = (peer[:, None] == peer[None, :]) & (order[None, :] < order[:, None])
    slot = peer * capacity + jnp.sum(earlier.astype(jnp.int32), axis=1)
    asked = jnp.sum(
        jnp.where(slot[None, :] == jnp.arange(peers * capacity)[:, None], run[None, :], 0), axis=1
    )
    wanted = lax.all_to_all(
        asked.reshape(peers, capacity), "dp", split_axis=0, concat_axis=0, tiled=True
    ).reshape(peers * capacity)

    aux_rows = side_rows(key_rows, query_rows, step_rows).reshape(runs, SEG, AUX)
    token_runs = token_rows.reshape(runs, SEG, whole_width)

    def exchange(block):
        rows = block.reshape(peers, capacity * SEG, block.shape[2])
        rows = lax.all_to_all(rows, "dp", split_axis=0, concat_axis=0, tiled=True)
        return rows.reshape(block.shape)

    widths = [n * head_width for n in PARTS]
    firsts = [sum(PARTS[:i]) for i in range(len(PARTS))]
    scalars = jnp.concatenate(
        [document_starts[0], (lax.axis_index("seq") * tokens).astype(jnp.int32)[None]]
    )
    decay_row = jnp.pad(decay_log, (0, LANES - heads))[None, :]
    skip_row = jnp.repeat(skip_gain, head_width)[None, :]
    query_at = 1
    parts = range(len(PARTS))

    sent = []
    for i in parts:
        sent.append(
            pick_runs(wanted, token_runs, firsts[i] * head_width, widths[i], None if i else aux_rows)
        )
        wanted, sent[i] = lax.optimization_barrier((wanted, sent[i]))
    got, arrived = [], []

    def work(i, result, with_end, with_local):
        return blocks(
            got[i], slot, widths[i], firsts[i], head_width, tables, aux, query_at, skip_row, result,
            whole_width, with_end, with_local,
        )

    def send_end(end):
        arrived.append([shifted(end, d) for d in range(1, shards)])

    def entering(i, result):
        return add_entering(
            result, widths[i], firsts[i], head_width, query_at, aux, tables[6], arrived[i]
        )

    got.append(exchange(sent[0]))
    got[0], sent[1] = lax.optimization_barrier((got[0], sent[1]))
    got.append(exchange(sent[1]))
    aux = pick_runs(slot, got[0], widths[0], AUX).reshape(tokens, AUX)
    tables = prepare(aux, 0, decay_row, scalars)
    end, result = work(0, None, True, True)
    send_end(end)
    result = entering(0, result)
    got[1], sent[2], result = lax.optimization_barrier((got[1], sent[2], result))
    got.append(exchange(sent[2]))
    (end,) = work(1, None, True, False)
    send_end(end)
    (result,) = work(1, result, False, True)
    (end,) = work(2, None, True, False)
    send_end(end)
    (result,) = work(2, result, False, True)
    result = entering(1, result)
    result = entering(2, result)
    return result[None]


def solution(mesh):
    in_specs = (
        P(("dp", "seq"), None),
        P(("dp", "seq"), None),
        P(("dp", "seq"), None),
        P(("dp", "seq"), None),
        P(),
        P(),
        P("dp", "seq"),
        P("dp", None),
    )
    out_specs = P("dp", "seq", None)
    return jax.shard_map(
        on_device, mesh=mesh, in_specs=in_specs, out_specs=out_specs, check_vma=False
    )
```

```python
import functools
import math

import jax
import jax.numpy as jnp
from jax import lax
from jax.experimental import pallas as pl
from jax.experimental.pallas import tpu as pltpu
from jax.sharding import PartitionSpec as P

SPAN = 256
SEG = 8
LANES = 128
AUX = 3 * LANES
GROUP = 16
PARTS = (32, 32, 16)
CHUNK = 16
LOG2E = math.log2(math.e)
CEILING = 64.0

f32 = jnp.float32
bf16 = jnp.bfloat16


def params(mib, *semantics):
    return pltpu.CompilerParams(vmem_limit_bytes=mib * 2**20, dimension_semantics=semantics or None)


def estimate(flops, moved, exps=0):
    return pl.CostEstimate(flops=int(flops), bytes_accessed=int(moved), transcendentals=int(exps))


def pick_runs(ids, source, first, width, extra=None):
    count = ids.shape[0]
    more = 0 if extra is None else extra.shape[2]
    sources = (source,) if extra is None else (source, extra)
    total = width + more
    chunk = max(n for n in range(1, CHUNK + 1) if count % n == 0)
    chunks = count // chunk

    def kernel(ids_ref, *refs):
        out_ref, held, in_sems, out_sems = refs[-4:]

        @pl.loop(0, chunks)
        def _(c):
            @pl.loop(0, chunk)
            def _(i):
                place = c * chunk + i
                run = ids_ref[place]
                pltpu.make_async_copy(
                    refs[0].at[run, :, pl.ds(first, width)],
                    held.at[place, :, pl.ds(0, width)],
                    in_sems.at[c],
                ).start()
                if more:
                    pltpu.make_async_copy(
                        refs[1].at[run], held.at[place, :, pl.ds(width, more)], in_sems.at[c]
                    ).start()

        @pl.loop(0, chunks)
        def _(c):
            part = pl.ds(c * chunk, chunk)
            pltpu.make_async_copy(held.at[part], held.at[part], in_sems.at[c]).wait()
            pltpu.make_async_copy(held.at[part], out_ref.at[part], out_sems.at[c]).start()

        @pl.loop(0, chunks)
        def _(c):
            part = pl.ds(c * chunk, chunk)
            pltpu.make_async_copy(held.at[part], out_ref.at[part], out_sems.at[c]).wait()

    return pl.pallas_call(
        kernel,
        out_shape=jax.ShapeDtypeStruct((count, SEG, total), source.dtype),
        grid_spec=pltpu.PrefetchScalarGridSpec(
            num_scalar_prefetch=1,
            grid=(1,),
            in_specs=[pl.BlockSpec(memory_space=pl.ANY)] * len(sources),
            out_specs=pl.BlockSpec(memory_space=pl.ANY),
            scratch_shapes=[
                pltpu.VMEM((count, SEG, total), source.dtype),
                pltpu.SemaphoreType.DMA((chunks,)),
                pltpu.SemaphoreType.DMA((chunks,)),
            ],
        ),
        compiler_params=params(56),
        cost_estimate=estimate(0, 4 * count * SEG * total),
    )(ids, *sources)


def side_rows(key_rows, query_rows, step_rows):
    tokens, heads = step_rows.shape

    def kernel(k_ref, q_ref, st_ref, out_ref):
        out_ref[:, 0:LANES] = k_ref[...]
        out_ref[:, LANES : 2 * LANES] = q_ref[...]
        steps = st_ref[...].astype(f32)
        steps = jnp.concatenate([steps, jnp.zeros((LANES - heads, tokens), f32)], axis=0)
        out_ref[:, 2 * LANES : AUX] = jnp.transpose(steps).astype(bf16)

    return pl.pallas_call(
        kernel,
        out_shape=jax.ShapeDtypeStruct((tokens, AUX), bf16),
        compiler_params=params(32),
        cost_estimate=estimate(0, 4 * tokens * AUX),
    )(key_rows, query_rows, step_rows.T)


def prepare(packed, columns, decay_row, scalars):
    tokens = packed.shape[0]
    spans = tokens // SPAN
    starts = scalars.shape[0] - 1

    def kernel(
        sc_ref, k_ref, q_ref, st_ref, dec_ref,
        cum_ref, rt_ref, score_ref, kt_ref, endw_ref, entry_ref, entd_ref, ret_ref, thru_ref, pref,
    ):
        j = pl.program_id(0)

        @pl.when(j == 0)
        def _():
            pref[...] = jnp.ones_like(pref)

        raw = st_ref[...].astype(f32)
        step = jnp.maximum(raw, 0.0) + jnp.log1p(jnp.exp(-jnp.abs(raw)))
        decay = step * (jnp.exp(dec_ref[...]) * (-LOG2E))
        row = lax.broadcasted_iota(jnp.int32, (SPAN, SPAN), 0)
        col = lax.broadcasted_iota(jnp.int32, (SPAN, SPAN), 1)
        tri = (col <= row).astype(f32)
        cum = jnp.dot(tri, decay, precision=lax.Precision.HIGHEST, preferred_element_type=f32)
        begin = sc_ref[starts] + j * SPAN
        doc_row = jnp.zeros((SPAN, SPAN), jnp.int32)
        doc_col = jnp.zeros((SPAN, SPAN), jnp.int32)
        doc_tok = jnp.zeros((SPAN, LANES), jnp.int32)
        token = lax.broadcasted_iota(jnp.int32, (SPAN, LANES), 0)
        doc_end = jnp.int32(0)
        for d in range(starts):
            at = sc_ref[d] - begin
            at = jnp.where(at < 0, SPAN, at)
            doc_row += (at <= row).astype(jnp.int32)
            doc_col += (at <= col).astype(jnp.int32)
            doc_tok += (at <= token).astype(jnp.int32)
            doc_end += (at < SPAN).astype(jnp.int32)
        linked = (doc_row == doc_col) & (col <= row)
        scores = lax.dot_general(
            q_ref[...], k_ref[...], (((1,), (1,)), ((), ())), preferred_element_type=f32
        )
        score_ref[0] = jnp.where(linked, scores, 0.0)
        last = cum[SPAN - 1 : SPAN, :]
        cum_ref[...] = cum
        rt_ref[0] = jnp.transpose(cum - jnp.log(step) * LOG2E)
        kt_ref[0] = jnp.transpose(k_ref[...].astype(f32)).astype(bf16)
        endw_ref[...] = jnp.where(doc_tok == doc_end, jnp.exp2(last - cum), 0.0) * step
        entry = jnp.where(doc_tok == 0, jnp.exp2(cum), 0.0)
        entry_ref[...] = entry
        entd_ref[...] = entry * pref[0:1, :]
        kept = jnp.where(doc_end == 0, jnp.exp2(last), 0.0)
        kept = jnp.broadcast_to(kept, (8, LANES))
        ret_ref[0] = kept
        pref[...] = pref[...] * kept
        thru_ref[...] = pref[...]

    block = columns // LANES
    span_rows = pl.BlockSpec((SPAN, LANES), lambda j, s: (j, 0))
    rows = jax.ShapeDtypeStruct((tokens, LANES), f32)
    return pl.pallas_call(
        kernel,
        out_shape=(
            rows,
            jax.ShapeDtypeStruct((spans, LANES, SPAN), f32),
            jax.ShapeDtypeStruct((spans, SPAN, SPAN), f32),
            jax.ShapeDtypeStruct((spans, LANES, SPAN), bf16),
            rows,
            rows,
            rows,
            jax.ShapeDtypeStruct((spans, 8, LANES), f32),
            jax.ShapeDtypeStruct((8, LANES), f32),
        ),
        grid_spec=pltpu.PrefetchScalarGridSpec(
            num_scalar_prefetch=1,
            grid=(spans,),
            in_specs=[
                pl.BlockSpec((SPAN, LANES), lambda j, s: (j, block)),
                pl.BlockSpec((SPAN, LANES), lambda j, s: (j, block + 1)),
                pl.BlockSpec((SPAN, LANES), lambda j, s: (j, block + 2)),
                pl.BlockSpec((1, LANES), lambda j, s: (0, 0)),
            ],
            out_specs=[
                span_rows,
                pl.BlockSpec((1, LANES, SPAN), lambda j, s: (j, 0, 0)),
                pl.BlockSpec((1, SPAN, SPAN), lambda j, s: (j, 0, 0)),
                pl.BlockSpec((1, LANES, SPAN), lambda j, s: (j, 0, 0)),
                span_rows,
                span_rows,
                span_rows,
                pl.BlockSpec((1, 8, LANES), lambda j, s: (j, 0, 0)),
                pl.BlockSpec((8, LANES), lambda j, s: (0, 0)),
            ],
            scratch_shapes=[pltpu.VMEM((8, LANES), f32)],
        ),
        compiler_params=params(56, "arbitrary"),
        cost_estimate=estimate(spans * 2 * SPAN * SPAN * LANES * 7, 6 * 2**20),
    )(scalars, packed, packed, packed, decay_row)


def spreader(width, head_width, first_head):
    lane = lax.broadcasted_iota(jnp.int32, (LANES, width), 1)
    start = (lax.broadcasted_iota(jnp.int32, (LANES, width), 0) - first_head) * head_width
    once = ((lane >= start) & (lane < start + head_width)).astype(f32).astype(bf16)
    return jnp.concatenate([once, once], axis=0)


def halves(x):
    high = x.astype(bf16)
    return high, (x - high.astype(f32)).astype(bf16)


def summands(table):
    return jnp.concatenate(halves(table), axis=1)


def spread(pair, matrix):
    return jnp.dot(pair, matrix, preferred_element_type=f32)


def blocks(
    got, slot, width, first_head, head_width, tables, aux, query_at, skip_row, result, whole_width, with_end, with_local
):
    cum, rt, scores, kt, endw, entry, _, ret, thru = tables
    tokens = slot.shape[0] * SEG
    spans = tokens // SPAN
    step_width = GROUP * head_width
    groups = width // step_width
    half = SPAN // 2
    runs = SPAN // SEG

    def kernel(slot_ref, *refs):
        refs = list(refs)
        got_ref, kt_ref, endw_ref, ret_ref, thru_ref = refs[:5]
        del refs[:5]
        if with_local:
            q_ref, cum_ref, rt_ref, score_ref, entry_ref, skip_ref = refs[:6]
            del refs[:6]
            if result is not None:
                del refs[:1]
        if with_end:
            final_ref = refs.pop(0)
        if with_local:
            out_ref = refs.pop(0)
            outs_held, out_sems = refs[-2:]
        state, matrix, held, sems = refs[:4]

        @pl.loop(0, spans)
        def _(j):
            @pl.loop(0, runs, unroll=8)
            def _(i):
                pltpu.make_async_copy(
                    got_ref.at[slot_ref[j * runs + i], :, pl.ds(0, width)], held.at[j, i], sems.at[j]
                ).start()

        state[...] = jnp.zeros_like(state)
        for g in range(groups):
            matrix[g] = spreader(step_width, head_width, first_head + g * GROUP)

        def written(j):
            return pltpu.make_async_copy(
                outs_held.at[lax.rem(j, 2)],
                out_ref.at[pl.ds(pl.multiple_of(j * SPAN, SPAN), SPAN), pl.ds(first_head * head_width, width)],
                out_sems.at[lax.rem(j, 2)],
            )

        @pl.loop(0, spans)
        def _(j):
            tokens_of = pl.ds(pl.multiple_of(j * SPAN, SPAN), SPAN)
            end_weight = summands(endw_ref[tokens_of, :])
            kept_all = summands(ret_ref[j])
            if with_local:
                entry_all = summands(entry_ref[tokens_of, :])
                query = q_ref[tokens_of, :]
                query = jnp.concatenate([query, query], axis=1)
                lane = lax.broadcasted_iota(jnp.int32, (half, 2 * head_width), 1)

                @pl.when(j >= 2)
                def _():
                    written(j - 2).wait()

            pltpu.make_async_copy(held.at[j], held.at[j], sems.at[j]).wait()

            for g in range(groups):
                head = first_head + g * GROUP
                columns = slice(g * step_width, (g + 1) * step_width)
                block = held[j, :, :, columns].reshape(SPAN, step_width)
                old = state[:, columns]
                scaled = block.astype(f32) * spread(end_weight, matrix[g])
                added = jnp.dot(kt_ref[j], scaled.astype(bf16), preferred_element_type=f32)
                state[:, columns] = spread(kept_all, matrix[g])[0:1, :] * old + added
                if not with_local:
                    continue
                base = jnp.dot(
                    query, jnp.concatenate(halves(old), axis=0), preferred_element_type=f32
                )
                base = base * spread(entry_all, matrix[g])
                skip = skip_ref[:, head * head_width : head * head_width + step_width]
                base = base + skip * block.astype(f32)
                for pair in range(GROUP // 2):
                    at = pair * 2 * head_width
                    values = block[:, at : at + 2 * head_width]
                    for part in range(2):
                        reach = (part + 1) * half
                        rows = slice(part * half, reach)
                        rows_of = pl.ds(pl.multiple_of(j * SPAN + part * half, half), half)
                        outs = []
                        for h in (head + 2 * pair, head + 2 * pair + 1):
                            gap = cum_ref[rows_of, h : h + 1] - rt_ref[j, h : h + 1, 0:reach]
                            gap = jnp.minimum(gap, CEILING)
                            weights = score_ref[j, rows, 0:reach] * jnp.exp2(gap)
                            outs.append(
                                jnp.dot(
                                    weights.astype(bf16), values[0:reach], preferred_element_type=f32
                                )
                            )
                        within = jnp.where(lane < head_width, outs[0], outs[1])
                        to = columns.start + at
                        outs_held[lax.rem(j, 2), rows, to : to + 2 * head_width] = (
                            within + base[rows, at : at + 2 * head_width]
                        ).astype(bf16)
            if with_local:
                written(j).start()

        if with_end:
            through_all = summands(thru_ref[...])
            for g in range(groups):
                columns = slice(g * step_width, (g + 1) * step_width)
                final_ref[0:LANES, columns] = state[:, columns].astype(bf16)
                high, low = halves(spread(through_all, matrix[g]))
                final_ref[LANES : LANES + 16, columns] = jnp.concatenate([high, low], axis=0)
        if with_local:
            for j in range(max(spans - 2, 0), spans):
                written(jnp.int32(j)).wait()

    def whole(array, columns=None, at=0):
        shape = array.shape if columns is None else array.shape[:-1] + (columns,)
        return pl.BlockSpec(shape, lambda i, s: (0,) * (len(shape) - 1) + (at,))

    anywhere = pl.BlockSpec(memory_space=pl.ANY)
    operands = [got, kt, endw, ret, thru]
    in_specs = [anywhere, whole(kt), whole(endw), whole(ret), whole(thru)]
    out_shape, out_specs, aliases = [], [], {}
    scratch = [
        pltpu.VMEM((LANES, width), f32),
        pltpu.VMEM((groups, 2 * LANES, step_width), bf16),
        pltpu.VMEM((spans, runs, SEG, width), bf16),
        pltpu.SemaphoreType.DMA((spans,)),
    ]
    if with_end:
        out_shape.append(jax.ShapeDtypeStruct((LANES + 16, width), bf16))
        out_specs.append(pl.BlockSpec((LANES + 16, width), lambda i, s: (0, 0)))
    if with_local:
        operands += [aux, cum, rt, scores, entry, skip_row]
        in_specs += [whole(aux, LANES, query_at), whole(cum), whole(rt), whole(scores), whole(entry)]
        in_specs.append(whole(skip_row))
        if result is not None:
            aliases = {1 + len(operands): len(out_shape)}
            operands.append(result)
            in_specs.append(anywhere)
        out_shape.append(jax.ShapeDtypeStruct((tokens, whole_width), bf16))
        out_specs.append(anywhere)
        scratch += [pltpu.VMEM((2, SPAN, width), bf16), pltpu.SemaphoreType.DMA((2,))]
    return pl.pallas_call(
        kernel,
        out_shape=tuple(out_shape),
        grid_spec=pltpu.PrefetchScalarGridSpec(
            num_scalar_prefetch=1,
            grid=(1,),
            in_specs=in_specs,
            out_specs=tuple(out_specs),
            scratch_shapes=scratch,
        ),
        input_output_aliases=aliases,
        compiler_params=params(56),
        cost_estimate=estimate(
            2 * tokens * width * (5 if with_local else 2) * SPAN,
            6 * tokens * width,
            tokens * SPAN * width // head_width if with_local else 0,
        ),
    )(slot, *operands)


def add_entering(result, width, first_head, head_width, query_at, aux, entd, arrived):
    tokens = result.shape[0]
    spans = tokens // SPAN
    step_width = GROUP * head_width
    groups = width // step_width

    def kernel(q_ref, entd_ref, *rest):
        froms = rest[: len(arrived)]
        in_ref, out_ref, matrix, state, held, in_sems, out_sems = rest[len(arrived) :]

        def place(ref, j):
            first = pl.multiple_of(j * SPAN, SPAN)
            return ref.at[pl.ds(first, SPAN), pl.ds(first_head * head_width, width)]

        @pl.loop(0, spans)
        def _(j):
            pltpu.make_async_copy(place(in_ref, j), held.at[j], in_sems.at[j]).start()

        for g in range(groups):
            matrix[g] = spreader(step_width, head_width, first_head + g * GROUP)
        incoming = froms[-1][0:LANES, :].astype(f32)
        for ref in reversed(froms[:-1]):
            factor = ref[LANES : LANES + 16, :].astype(f32)
            incoming = ref[0:LANES, :].astype(f32) + (factor[0:1, :] + factor[8:9, :]) * incoming
        state[...] = incoming.astype(bf16)

        @pl.loop(0, spans)
        def _(j):
            tokens_of = pl.ds(pl.multiple_of(j * SPAN, SPAN), SPAN)
            entry_all = summands(entd_ref[tokens_of, :])
            pltpu.make_async_copy(place(in_ref, j), held.at[j], in_sems.at[j]).wait()
            for g in range(groups):
                columns = slice(g * step_width, (g + 1) * step_width)
                part = jnp.dot(
                    q_ref[tokens_of, :], state[:, columns], preferred_element_type=f32
                )
                part = part * spread(entry_all, matrix[g])
                held[j, :, columns] = (held[j, :, columns].astype(f32) + part).astype(bf16)
            pltpu.make_async_copy(held.at[j], place(out_ref, j), out_sems.at[j]).start()

        @pl.loop(0, spans)
        def _(j):
            pltpu.make_async_copy(held.at[j], place(out_ref, j), out_sems.at[j]).wait()

    return pl.pallas_call(
        kernel,
        out_shape=jax.ShapeDtypeStruct(result.shape, result.dtype),
        grid=(1,),
        in_specs=[
            pl.BlockSpec((tokens, LANES), lambda i: (0, query_at)),
            pl.BlockSpec((tokens, LANES), lambda i: (0, 0)),
        ]
        + [pl.BlockSpec((LANES + 16, width), lambda i: (0, 0))] * len(arrived)
        + [pl.BlockSpec(memory_space=pl.ANY)],
        out_specs=pl.BlockSpec(memory_space=pl.ANY),
        scratch_shapes=[
            pltpu.VMEM((groups, 2 * LANES, step_width), bf16),
            pltpu.VMEM((LANES, width), bf16),
            pltpu.VMEM((spans, SPAN, width), bf16),
            pltpu.SemaphoreType.DMA((spans,)),
            pltpu.SemaphoreType.DMA((spans,)),
        ],
        input_output_aliases={2 + len(arrived): 0},
        compiler_params=params(56),
        cost_estimate=estimate(2 * tokens * width * 3 * LANES, 4 * tokens * width),
    )(aux, entd, *arrived, result)


def shifted(block, distance):
    count = lax.axis_size("seq")
    return lax.ppermute(block, "seq", [(i, i + distance) for i in range(count - distance)])


def on_device(
    token_rows, key_rows, query_rows, step_rows, decay_log, skip_gain, source_rows, document_starts
):
    tokens, whole_width = token_rows.shape
    peers = lax.axis_size("dp")
    shards = lax.axis_size("seq")
    heads = decay_log.shape[0]
    head_width = whole_width // heads
    runs = tokens // SEG
    capacity = runs // peers + 1

    first_rows = source_rows[0].reshape(runs, SEG)[:, 0]
    peer = first_rows // (tokens * shards)
    run = (first_rows % tokens) // SEG
    order = jnp.arange(runs)
    earlier = (peer[:, None] == peer[None, :]) & (order[None, :] < order[:, None])
    slot = peer * capacity + jnp.sum(earlier.astype(jnp.int32), axis=1)
    asked = jnp.sum(
        jnp.where(slot[None, :] == jnp.arange(peers * capacity)[:, None], run[None, :], 0), axis=1
    )
    wanted = lax.all_to_all(
        asked.reshape(peers, capacity), "dp", split_axis=0, concat_axis=0, tiled=True
    ).reshape(peers * capacity)

    aux_rows = side_rows(key_rows, query_rows, step_rows).reshape(runs, SEG, AUX)
    token_runs = token_rows.reshape(runs, SEG, whole_width)

    def exchange(block):
        rows = block.reshape(peers, capacity * SEG, block.shape[2])
        rows = lax.all_to_all(rows, "dp", split_axis=0, concat_axis=0, tiled=True)
        return rows.reshape(block.shape)

    widths = [n * head_width for n in PARTS]
    firsts = [sum(PARTS[:i]) for i in range(len(PARTS))]
    scalars = jnp.concatenate(
        [document_starts[0], (lax.axis_index("seq") * tokens).astype(jnp.int32)[None]]
    )
    decay_row = jnp.pad(decay_log, (0, LANES - heads))[None, :]
    skip_row = jnp.repeat(skip_gain, head_width)[None, :]
    query_at = 1
    parts = range(len(PARTS))

    sent = []
    for i in parts:
        sent.append(
            pick_runs(wanted, token_runs, firsts[i] * head_width, widths[i], None if i else aux_rows)
        )
        wanted, sent[i] = lax.optimization_barrier((wanted, sent[i]))
    got, arrived = [], []

    def work(i, result, with_end, with_local):
        return blocks(
            got[i], slot, widths[i], firsts[i], head_width, tables, aux, query_at, skip_row, result,
            whole_width, with_end, with_local,
        )

    def send_end(end):
        arrived.append([shifted(end, d) for d in range(1, shards)])

    def entering(i, result):
        return add_entering(
            result, widths[i], firsts[i], head_width, query_at, aux, tables[6], arrived[i]
        )

    got.append(exchange(sent[0]))
    got[0], sent[1] = lax.optimization_barrier((got[0], sent[1]))
    got.append(exchange(sent[1]))
    aux = pick_runs(slot, got[0], widths[0], AUX).reshape(tokens, AUX)
    tables = prepare(aux, 0, decay_row, scalars)
    end, result = work(0, None, True, True)
    send_end(end)
    result = entering(0, result)
    got[1], sent[2], result = lax.optimization_barrier((got[1], sent[2], result))
    got.append(exchange(sent[2]))
    end, result = work(1, result, True, True)
    send_end(end)
    (end,) = work(2, None, True, False)
    send_end(end)
    (result,) = work(2, result, False, True)
    result = entering(1, result)
    result = entering(2, result)
    return result[None]


def solution(mesh):
    in_specs = (
        P(("dp", "seq"), None),
        P(("dp", "seq"), None),
        P(("dp", "seq"), None),
        P(("dp", "seq"), None),
        P(),
        P(),
        P("dp", "seq"),
        P("dp", None),
    )
    out_specs = P("dp", "seq", None)
    return jax.shard_map(
        on_device, mesh=mesh, in_specs=in_specs, out_specs=out_specs, check_vma=False
    )
```

```python
import functools
import math

import jax
import jax.numpy as jnp
from jax import lax
from jax.experimental import pallas as pl
from jax.experimental.pallas import tpu as pltpu
from jax.sharding import PartitionSpec as P

SPAN = 256
SEG = 8
LANES = 128
AUX = 3 * LANES
GROUP = 8
PARTS = (40, 32, 8)
CHUNK = 16
LOG2E = math.log2(math.e)
CEILING = 64.0

f32 = jnp.float32
bf16 = jnp.bfloat16


def params(mib, *semantics):
    return pltpu.CompilerParams(vmem_limit_bytes=mib * 2**20, dimension_semantics=semantics or None)


def estimate(flops, moved, exps=0):
    return pl.CostEstimate(flops=int(flops), bytes_accessed=int(moved), transcendentals=int(exps))


def pick_runs(ids, source, first, width, extra=None):
    count = ids.shape[0]
    more = 0 if extra is None else extra.shape[2]
    sources = (source,) if extra is None else (source, extra)
    total = width + more
    chunk = max(n for n in range(1, CHUNK + 1) if count % n == 0)
    chunks = count // chunk

    def kernel(ids_ref, *refs):
        out_ref, held, in_sems, out_sems = refs[-4:]

        @pl.loop(0, chunks)
        def _(c):
            @pl.loop(0, chunk)
            def _(i):
                place = c * chunk + i
                run = ids_ref[place]
                pltpu.make_async_copy(
                    refs[0].at[run, :, pl.ds(first, width)],
                    held.at[place, :, pl.ds(0, width)],
                    in_sems.at[c],
                ).start()
                if more:
                    pltpu.make_async_copy(
                        refs[1].at[run], held.at[place, :, pl.ds(width, more)], in_sems.at[c]
                    ).start()

        @pl.loop(0, chunks)
        def _(c):
            part = pl.ds(c * chunk, chunk)
            pltpu.make_async_copy(held.at[part], held.at[part], in_sems.at[c]).wait()
            pltpu.make_async_copy(held.at[part], out_ref.at[part], out_sems.at[c]).start()

        @pl.loop(0, chunks)
        def _(c):
            part = pl.ds(c * chunk, chunk)
            pltpu.make_async_copy(held.at[part], out_ref.at[part], out_sems.at[c]).wait()

    return pl.pallas_call(
        kernel,
        out_shape=jax.ShapeDtypeStruct((count, SEG, total), source.dtype),
        grid_spec=pltpu.PrefetchScalarGridSpec(
            num_scalar_prefetch=1,
            grid=(1,),
            in_specs=[pl.BlockSpec(memory_space=pl.ANY)] * len(sources),
            out_specs=pl.BlockSpec(memory_space=pl.ANY),
            scratch_shapes=[
                pltpu.VMEM((count, SEG, total), source.dtype),
                pltpu.SemaphoreType.DMA((chunks,)),
                pltpu.SemaphoreType.DMA((chunks,)),
            ],
        ),
        compiler_params=params(56),
        cost_estimate=estimate(0, 4 * count * SEG * total),
    )(ids, *sources)


def side_rows(key_rows, query_rows, step_rows):
    tokens, heads = step_rows.shape

    def kernel(k_ref, q_ref, st_ref, out_ref):
        out_ref[:, 0:LANES] = k_ref[...]
        out_ref[:, LANES : 2 * LANES] = q_ref[...]
        steps = st_ref[...].astype(f32)
        steps = jnp.concatenate([steps, jnp.zeros((LANES - heads, tokens), f32)], axis=0)
        out_ref[:, 2 * LANES : AUX] = jnp.transpose(steps).astype(bf16)

    return pl.pallas_call(
        kernel,
        out_shape=jax.ShapeDtypeStruct((tokens, AUX), bf16),
        compiler_params=params(32),
        cost_estimate=estimate(0, 4 * tokens * AUX),
    )(key_rows, query_rows, step_rows.T)


def prepare(packed, columns, decay_row, scalars):
    tokens = packed.shape[0]
    spans = tokens // SPAN
    starts = scalars.shape[0] - 1

    def kernel(
        sc_ref, k_ref, q_ref, st_ref, dec_ref,
        cum_ref, rt_ref, score_ref, kt_ref, endw_ref, entry_ref, entd_ref, ret_ref, thru_ref, pref,
    ):
        j = pl.program_id(0)

        @pl.when(j == 0)
        def _():
            pref[...] = jnp.ones_like(pref)

        raw = st_ref[...].astype(f32)
        step = jnp.maximum(raw, 0.0) + jnp.log1p(jnp.exp(-jnp.abs(raw)))
        decay = step * (jnp.exp(dec_ref[...]) * (-LOG2E))
        row = lax.broadcasted_iota(jnp.int32, (SPAN, SPAN), 0)
        col = lax.broadcasted_iota(jnp.int32, (SPAN, SPAN), 1)
        tri = (col <= row).astype(f32)
        cum = jnp.dot(tri, decay, precision=lax.Precision.HIGHEST, preferred_element_type=f32)
        begin = sc_ref[starts] + j * SPAN
        doc_row = jnp.zeros((SPAN, SPAN), jnp.int32)
        doc_col = jnp.zeros((SPAN, SPAN), jnp.int32)
        doc_tok = jnp.zeros((SPAN, LANES), jnp.int32)
        token = lax.broadcasted_iota(jnp.int32, (SPAN, LANES), 0)
        doc_end = jnp.int32(0)
        for d in range(starts):
            at = sc_ref[d] - begin
            at = jnp.where(at < 0, SPAN, at)
            doc_row += (at <= row).astype(jnp.int32)
            doc_col += (at <= col).astype(jnp.int32)
            doc_tok += (at <= token).astype(jnp.int32)
            doc_end += (at < SPAN).astype(jnp.int32)
        linked = (doc_row == doc_col) & (col <= row)
        scores = lax.dot_general(
            q_ref[...], k_ref[...], (((1,), (1,)), ((), ())), preferred_element_type=f32
        )
        score_ref[0] = jnp.where(linked, scores, 0.0)
        last = cum[SPAN - 1 : SPAN, :]
        cum_ref[...] = cum
        rt_ref[0] = jnp.transpose(cum - jnp.log(step) * LOG2E)
        kt_ref[0] = jnp.transpose(k_ref[...].astype(f32)).astype(bf16)
        endw_ref[...] = jnp.where(doc_tok == doc_end, jnp.exp2(last - cum), 0.0) * step
        entry = jnp.where(doc_tok == 0, jnp.exp2(cum), 0.0)
        entry_ref[...] = entry
        entd_ref[...] = entry * pref[0:1, :]
        kept = jnp.where(doc_end == 0, jnp.exp2(last), 0.0)
        kept = jnp.broadcast_to(kept, (8, LANES))
        ret_ref[0] = kept
        pref[...] = pref[...] * kept
        thru_ref[...] = pref[...]

    block = columns // LANES
    span_rows = pl.BlockSpec((SPAN, LANES), lambda j, s: (j, 0))
    rows = jax.ShapeDtypeStruct((tokens, LANES), f32)
    return pl.pallas_call(
        kernel,
        out_shape=(
            rows,
            jax.ShapeDtypeStruct((spans, LANES, SPAN), f32),
            jax.ShapeDtypeStruct((spans, SPAN, SPAN), f32),
            jax.ShapeDtypeStruct((spans, LANES, SPAN), bf16),
            rows,
            rows,
            rows,
            jax.ShapeDtypeStruct((spans, 8, LANES), f32),
            jax.ShapeDtypeStruct((8, LANES), f32),
        ),
        grid_spec=pltpu.PrefetchScalarGridSpec(
            num_scalar_prefetch=1,
            grid=(spans,),
            in_specs=[
                pl.BlockSpec((SPAN, LANES), lambda j, s: (j, block)),
                pl.BlockSpec((SPAN, LANES), lambda j, s: (j, block + 1)),
                pl.BlockSpec((SPAN, LANES), lambda j, s: (j, block + 2)),
                pl.BlockSpec((1, LANES), lambda j, s: (0, 0)),
            ],
            out_specs=[
                span_rows,
                pl.BlockSpec((1, LANES, SPAN), lambda j, s: (j, 0, 0)),
                pl.BlockSpec((1, SPAN, SPAN), lambda j, s: (j, 0, 0)),
                pl.BlockSpec((1, LANES, SPAN), lambda j, s: (j, 0, 0)),
                span_rows,
                span_rows,
                span_rows,
                pl.BlockSpec((1, 8, LANES), lambda j, s: (j, 0, 0)),
                pl.BlockSpec((8, LANES), lambda j, s: (0, 0)),
            ],
            scratch_shapes=[pltpu.VMEM((8, LANES), f32)],
        ),
        compiler_params=params(56, "arbitrary"),
        cost_estimate=estimate(spans * 2 * SPAN * SPAN * LANES * 7, 6 * 2**20),
    )(scalars, packed, packed, packed, decay_row)


def spreader(width, head_width, first_head):
    lane = lax.broadcasted_iota(jnp.int32, (LANES, width), 1)
    start = (lax.broadcasted_iota(jnp.int32, (LANES, width), 0) - first_head) * head_width
    once = ((lane >= start) & (lane < start + head_width)).astype(f32).astype(bf16)
    return jnp.concatenate([once, once], axis=0)


def halves(x):
    high = x.astype(bf16)
    return high, (x - high.astype(f32)).astype(bf16)


def summands(table):
    return jnp.concatenate(halves(table), axis=1)


def spread(pair, matrix):
    return jnp.dot(pair, matrix, preferred_element_type=f32)


def blocks(
    got, slot, width, first_head, head_width, tables, aux, query_at, skip_row, result, whole_width, with_end, with_local
):
    cum, rt, scores, kt, endw, entry, _, ret, thru = tables
    tokens = slot.shape[0] * SEG
    spans = tokens // SPAN
    step_width = GROUP * head_width
    groups = width // step_width
    half = SPAN // 2
    runs = SPAN // SEG

    def kernel(slot_ref, *refs):
        refs = list(refs)
        got_ref, kt_ref, endw_ref, ret_ref, thru_ref = refs[:5]
        del refs[:5]
        if with_local:
            q_ref, cum_ref, rt_ref, score_ref, entry_ref, skip_ref = refs[:6]
            del refs[:6]
            if result is not None:
                del refs[:1]
        if with_end:
            final_ref = refs.pop(0)
        if with_local:
            out_ref = refs.pop(0)
            outs_held, out_sems = refs[-2:]
        state, matrix, held, sems = refs[:4]

        @pl.loop(0, spans)
        def _(j):
            @pl.loop(0, runs, unroll=8)
            def _(i):
                pltpu.make_async_copy(
                    got_ref.at[slot_ref[j * runs + i], :, pl.ds(0, width)], held.at[j, i], sems.at[j]
                ).start()

        state[...] = jnp.zeros_like(state)
        for g in range(groups):
            matrix[g] = spreader(step_width, head_width, first_head + g * GROUP)

        def written(j):
            return pltpu.make_async_copy(
                outs_held.at[lax.rem(j, 2)],
                out_ref.at[pl.ds(pl.multiple_of(j * SPAN, SPAN), SPAN), pl.ds(first_head * head_width, width)],
                out_sems.at[lax.rem(j, 2)],
            )

        @pl.loop(0, spans)
        def _(j):
            tokens_of = pl.ds(pl.multiple_of(j * SPAN, SPAN), SPAN)
            end_weight = summands(endw_ref[tokens_of, :])
            kept_all = summands(ret_ref[j])
            if with_local:
                entry_all = summands(entry_ref[tokens_of, :])
                query = q_ref[tokens_of, :]
                query = jnp.concatenate([query, query], axis=1)
                lane = lax.broadcasted_iota(jnp.int32, (half, 2 * head_width), 1)

                @pl.when(j >= 2)
                def _():
                    written(j - 2).wait()

            pltpu.make_async_copy(held.at[j], held.at[j], sems.at[j]).wait()

            for g in range(groups):
                head = first_head + g * GROUP
                columns = slice(g * step_width, (g + 1) * step_width)
                block = held[j, :, :, columns].reshape(SPAN, step_width)
                old = state[:, columns]
                scaled = block.astype(f32) * spread(end_weight, matrix[g])
                added = jnp.dot(kt_ref[j], scaled.astype(bf16), preferred_element_type=f32)
                state[:, columns] = spread(kept_all, matrix[g])[0:1, :] * old + added
                if not with_local:
                    continue
                base = jnp.dot(
                    query, jnp.concatenate(halves(old), axis=0), preferred_element_type=f32
                )
                base = base * spread(entry_all, matrix[g])
                skip = skip_ref[:, head * head_width : head * head_width + step_width]
                base = base + skip * block.astype(f32)
                for pair in range(GROUP // 2):
                    at = pair * 2 * head_width
                    values = block[:, at : at + 2 * head_width]
                    for part in range(2):
                        reach = (part + 1) * half
                        rows = slice(part * half, reach)
                        rows_of = pl.ds(pl.multiple_of(j * SPAN + part * half, half), half)
                        outs = []
                        for h in (head + 2 * pair, head + 2 * pair + 1):
                            gap = cum_ref[rows_of, h : h + 1] - rt_ref[j, h : h + 1, 0:reach]
                            gap = jnp.minimum(gap, CEILING)
                            weights = score_ref[j, rows, 0:reach] * jnp.exp2(gap)
                            outs.append(
                                jnp.dot(
                                    weights.astype(bf16), values[0:reach], preferred_element_type=f32
                                )
                            )
                        within = jnp.where(lane < head_width, outs[0], outs[1])
                        to = columns.start + at
                        outs_held[lax.rem(j, 2), rows, to : to + 2 * head_width] = (
                            within + base[rows, at : at + 2 * head_width]
                        ).astype(bf16)
            if with_local:
                written(j).start()

        if with_end:
            through_all = summands(thru_ref[...])
            for g in range(groups):
                columns = slice(g * step_width, (g + 1) * step_width)
                final_ref[0:LANES, columns] = state[:, columns].astype(bf16)
                high, low = halves(spread(through_all, matrix[g]))
                final_ref[LANES : LANES + 16, columns] = jnp.concatenate([high, low], axis=0)
        if with_local:
            for j in range(max(spans - 2, 0), spans):
                written(jnp.int32(j)).wait()

    def whole(array, columns=None, at=0):
        shape = array.shape if columns is None else array.shape[:-1] + (columns,)
        return pl.BlockSpec(shape, lambda i, s: (0,) * (len(shape) - 1) + (at,))

    anywhere = pl.BlockSpec(memory_space=pl.ANY)
    operands = [got, kt, endw, ret, thru]
    in_specs = [anywhere, whole(kt), whole(endw), whole(ret), whole(thru)]
    out_shape, out_specs, aliases = [], [], {}
    scratch = [
        pltpu.VMEM((LANES, width), f32),
        pltpu.VMEM((groups, 2 * LANES, step_width), bf16),
        pltpu.VMEM((spans, runs, SEG, width), bf16),
        pltpu.SemaphoreType.DMA((spans,)),
    ]
    if with_end:
        out_shape.append(jax.ShapeDtypeStruct((LANES + 16, width), bf16))
        out_specs.append(pl.BlockSpec((LANES + 16, width), lambda i, s: (0, 0)))
    if with_local:
        operands += [aux, cum, rt, scores, entry, skip_row]
        in_specs += [whole(aux, LANES, query_at), whole(cum), whole(rt), whole(scores), whole(entry)]
        in_specs.append(whole(skip_row))
        if result is not None:
            aliases = {1 + len(operands): len(out_shape)}
            operands.append(result)
            in_specs.append(anywhere)
        out_shape.append(jax.ShapeDtypeStruct((tokens, whole_width), bf16))
        out_specs.append(anywhere)
        scratch += [pltpu.VMEM((2, SPAN, width), bf16), pltpu.SemaphoreType.DMA((2,))]
    return pl.pallas_call(
        kernel,
        out_shape=tuple(out_shape),
        grid_spec=pltpu.PrefetchScalarGridSpec(
            num_scalar_prefetch=1,
            grid=(1,),
            in_specs=in_specs,
            out_specs=tuple(out_specs),
            scratch_shapes=scratch,
        ),
        input_output_aliases=aliases,
        compiler_params=params(56),
        cost_estimate=estimate(
            2 * tokens * width * (5 if with_local else 2) * SPAN,
            6 * tokens * width,
            tokens * SPAN * width // head_width if with_local else 0,
        ),
    )(slot, *operands)


def add_entering(result, width, first_head, head_width, query_at, aux, entd, arrived):
    tokens = result.shape[0]
    spans = tokens // SPAN
    step_width = GROUP * head_width
    groups = width // step_width

    def kernel(q_ref, entd_ref, *rest):
        froms = rest[: len(arrived)]
        in_ref, out_ref, matrix, state, held, in_sems, out_sems = rest[len(arrived) :]

        def place(ref, j):
            first = pl.multiple_of(j * SPAN, SPAN)
            return ref.at[pl.ds(first, SPAN), pl.ds(first_head * head_width, width)]

        @pl.loop(0, spans)
        def _(j):
            pltpu.make_async_copy(place(in_ref, j), held.at[j], in_sems.at[j]).start()

        for g in range(groups):
            matrix[g] = spreader(step_width, head_width, first_head + g * GROUP)
        incoming = froms[-1][0:LANES, :].astype(f32)
        for ref in reversed(froms[:-1]):
            factor = ref[LANES : LANES + 16, :].astype(f32)
            incoming = ref[0:LANES, :].astype(f32) + (factor[0:1, :] + factor[8:9, :]) * incoming
        state[...] = incoming.astype(bf16)

        @pl.loop(0, spans)
        def _(j):
            tokens_of = pl.ds(pl.multiple_of(j * SPAN, SPAN), SPAN)
            entry_all = summands(entd_ref[tokens_of, :])
            pltpu.make_async_copy(place(in_ref, j), held.at[j], in_sems.at[j]).wait()
            for g in range(groups):
                columns = slice(g * step_width, (g + 1) * step_width)
                part = jnp.dot(
                    q_ref[tokens_of, :], state[:, columns], preferred_element_type=f32
                )
                part = part * spread(entry_all, matrix[g])
                held[j, :, columns] = (held[j, :, columns].astype(f32) + part).astype(bf16)
            pltpu.make_async_copy(held.at[j], place(out_ref, j), out_sems.at[j]).start()

        @pl.loop(0, spans)
        def _(j):
            pltpu.make_async_copy(held.at[j], place(out_ref, j), out_sems.at[j]).wait()

    return pl.pallas_call(
        kernel,
        out_shape=jax.ShapeDtypeStruct(result.shape, result.dtype),
        grid=(1,),
        in_specs=[
            pl.BlockSpec((tokens, LANES), lambda i: (0, query_at)),
            pl.BlockSpec((tokens, LANES), lambda i: (0, 0)),
        ]
        + [pl.BlockSpec((LANES + 16, width), lambda i: (0, 0))] * len(arrived)
        + [pl.BlockSpec(memory_space=pl.ANY)],
        out_specs=pl.BlockSpec(memory_space=pl.ANY),
        scratch_shapes=[
            pltpu.VMEM((groups, 2 * LANES, step_width), bf16),
            pltpu.VMEM((LANES, width), bf16),
            pltpu.VMEM((spans, SPAN, width), bf16),
            pltpu.SemaphoreType.DMA((spans,)),
            pltpu.SemaphoreType.DMA((spans,)),
        ],
        input_output_aliases={2 + len(arrived): 0},
        compiler_params=params(56),
        cost_estimate=estimate(2 * tokens * width * 3 * LANES, 4 * tokens * width),
    )(aux, entd, *arrived, result)


def shifted(block, distance):
    count = lax.axis_size("seq")
    return lax.ppermute(block, "seq", [(i, i + distance) for i in range(count - distance)])


def on_device(
    token_rows, key_rows, query_rows, step_rows, decay_log, skip_gain, source_rows, document_starts
):
    tokens, whole_width = token_rows.shape
    peers = lax.axis_size("dp")
    shards = lax.axis_size("seq")
    heads = decay_log.shape[0]
    head_width = whole_width // heads
    runs = tokens // SEG
    capacity = runs // peers + 1

    first_rows = source_rows[0].reshape(runs, SEG)[:, 0]
    peer = first_rows // (tokens * shards)
    run = (first_rows % tokens) // SEG
    order = jnp.arange(runs)
    earlier = (peer[:, None] == peer[None, :]) & (order[None, :] < order[:, None])
    slot = peer * capacity + jnp.sum(earlier.astype(jnp.int32), axis=1)
    asked = jnp.sum(
        jnp.where(slot[None, :] == jnp.arange(peers * capacity)[:, None], run[None, :], 0), axis=1
    )
    wanted = lax.all_to_all(
        asked.reshape(peers, capacity), "dp", split_axis=0, concat_axis=0, tiled=True
    ).reshape(peers * capacity)

    aux_rows = side_rows(key_rows, query_rows, step_rows).reshape(runs, SEG, AUX)
    token_runs = token_rows.reshape(runs, SEG, whole_width)

    def exchange(block):
        rows = block.reshape(peers, capacity * SEG, block.shape[2])
        rows = lax.all_to_all(rows, "dp", split_axis=0, concat_axis=0, tiled=True)
        return rows.reshape(block.shape)

    widths = [n * head_width for n in PARTS]
    firsts = [sum(PARTS[:i]) for i in range(len(PARTS))]
    scalars = jnp.concatenate(
        [document_starts[0], (lax.axis_index("seq") * tokens).astype(jnp.int32)[None]]
    )
    decay_row = jnp.pad(decay_log, (0, LANES - heads))[None, :]
    skip_row = jnp.repeat(skip_gain, head_width)[None, :]
    query_at = 1
    parts = range(len(PARTS))

    sent = []
    for i in parts:
        sent.append(
            pick_runs(wanted, token_runs, firsts[i] * head_width, widths[i], None if i else aux_rows)
        )
        wanted, sent[i] = lax.optimization_barrier((wanted, sent[i]))
    got, arrived = [], []

    def work(i, result, with_end, with_local):
        return blocks(
            got[i], slot, widths[i], firsts[i], head_width, tables, aux, query_at, skip_row, result,
            whole_width, with_end, with_local,
        )

    def send_end(end):
        arrived.append([shifted(end, d) for d in range(1, shards)])

    def entering(i, result):
        return add_entering(
            result, widths[i], firsts[i], head_width, query_at, aux, tables[6], arrived[i]
        )

    got.append(exchange(sent[0]))
    got[0], sent[1] = lax.optimization_barrier((got[0], sent[1]))
    got.append(exchange(sent[1]))
    aux = pick_runs(slot, got[0], widths[0], AUX).reshape(tokens, AUX)
    tables = prepare(aux, 0, decay_row, scalars)
    (end,) = work(0, None, True, False)
    send_end(end)
    (result,) = work(0, None, False, True)
    result = entering(0, result)
    got[1], sent[2], result = lax.optimization_barrier((got[1], sent[2], result))
    got.append(exchange(sent[2]))
    (end,) = work(1, None, True, False)
    send_end(end)
    (result,) = work(1, result, False, True)
    end, result = work(2, result, True, True)
    send_end(end)
    result = entering(1, result)
    result = entering(2, result)
    return result[None]


def solution(mesh):
    in_specs = (
        P(("dp", "seq"), None),
        P(("dp", "seq"), None),
        P(("dp", "seq"), None),
        P(("dp", "seq"), None),
        P(),
        P(),
        P("dp", "seq"),
        P("dp", None),
    )
    out_specs = P("dp", "seq", None)
    return jax.shard_map(
        on_device, mesh=mesh, in_specs=in_specs, out_specs=out_specs, check_vma=False
    )
```

```python
import functools
import math

import jax
import jax.numpy as jnp
from jax import lax
from jax.experimental import pallas as pl
from jax.experimental.pallas import tpu as pltpu
from jax.sharding import PartitionSpec as P

SPAN = 256
SEG = 8
LANES = 128
AUX = 3 * LANES
GROUP = 16
PARTS = (32, 32, 16)
CHUNK = 16
LOG2E = math.log2(math.e)
CEILING = 64.0

f32 = jnp.float32
bf16 = jnp.bfloat16


def params(mib, *semantics):
    return pltpu.CompilerParams(vmem_limit_bytes=mib * 2**20, dimension_semantics=semantics or None)


def estimate(flops, moved, exps=0):
    return pl.CostEstimate(flops=int(flops), bytes_accessed=int(moved), transcendentals=int(exps))


def pick_runs(ids, source, first, width, extra=None):
    count = ids.shape[0]
    more = 0 if extra is None else extra.shape[2]
    sources = (source,) if extra is None else (source, extra)
    total = width + more
    chunk = max(n for n in range(1, CHUNK + 1) if count % n == 0)
    chunks = count // chunk

    def kernel(ids_ref, *refs):
        out_ref, held, in_sems, out_sems = refs[-4:]

        @pl.loop(0, chunks)
        def _(c):
            @pl.loop(0, chunk, unroll=chunk)
            def _(i):
                place = c * chunk + i
                run = ids_ref[place]
                pltpu.make_async_copy(
                    refs[0].at[run, :, pl.ds(first, width)],
                    held.at[place, :, pl.ds(0, width)],
                    in_sems.at[c],
                ).start()
                if more:
                    pltpu.make_async_copy(
                        refs[1].at[run], held.at[place, :, pl.ds(width, more)], in_sems.at[c]
                    ).start()

        @pl.loop(0, chunks)
        def _(c):
            part = pl.ds(c * chunk, chunk)
            pltpu.make_async_copy(held.at[part], held.at[part], in_sems.at[c]).wait()
            pltpu.make_async_copy(held.at[part], out_ref.at[part], out_sems.at[c]).start()

        @pl.loop(0, chunks)
        def _(c):
            part = pl.ds(c * chunk, chunk)
            pltpu.make_async_copy(held.at[part], out_ref.at[part], out_sems.at[c]).wait()

    return pl.pallas_call(
        kernel,
        out_shape=jax.ShapeDtypeStruct((count, SEG, total), source.dtype),
        grid_spec=pltpu.PrefetchScalarGridSpec(
            num_scalar_prefetch=1,
            grid=(1,),
            in_specs=[pl.BlockSpec(memory_space=pl.ANY)] * len(sources),
            out_specs=pl.BlockSpec(memory_space=pl.ANY),
            scratch_shapes=[
                pltpu.VMEM((count, SEG, total), source.dtype),
                pltpu.SemaphoreType.DMA((chunks,)),
                pltpu.SemaphoreType.DMA((chunks,)),
            ],
        ),
        compiler_params=params(56),
        cost_estimate=estimate(0, 4 * count * SEG * total),
    )(ids, *sources)


def side_rows(key_rows, query_rows, step_rows):
    tokens, heads = step_rows.shape

    def kernel(k_ref, q_ref, st_ref, out_ref):
        out_ref[:, 0:LANES] = k_ref[...]
        out_ref[:, LANES : 2 * LANES] = q_ref[...]
        steps = st_ref[...].astype(f32)
        steps = jnp.concatenate([steps, jnp.zeros((LANES - heads, tokens), f32)], axis=0)
        out_ref[:, 2 * LANES : AUX] = jnp.transpose(steps).astype(bf16)

    return pl.pallas_call(
        kernel,
        out_shape=jax.ShapeDtypeStruct((tokens, AUX), bf16),
        compiler_params=params(32),
        cost_estimate=estimate(0, 4 * tokens * AUX),
    )(key_rows, query_rows, step_rows.T)


def prepare(packed, columns, decay_row, scalars):
    tokens = packed.shape[0]
    spans = tokens // SPAN
    starts = scalars.shape[0] - 1

    def kernel(
        sc_ref, k_ref, q_ref, st_ref, dec_ref,
        cum_ref, rt_ref, score_ref, kt_ref, endw_ref, entry_ref, entd_ref, ret_ref, thru_ref, pref,
    ):
        j = pl.program_id(0)

        @pl.when(j == 0)
        def _():
            pref[...] = jnp.ones_like(pref)

        raw = st_ref[...].astype(f32)
        step = jnp.maximum(raw, 0.0) + jnp.log1p(jnp.exp(-jnp.abs(raw)))
        decay = step * (jnp.exp(dec_ref[...]) * (-LOG2E))
        row = lax.broadcasted_iota(jnp.int32, (SPAN, SPAN), 0)
        col = lax.broadcasted_iota(jnp.int32, (SPAN, SPAN), 1)
        tri = (col <= row).astype(f32)
        cum = jnp.dot(tri, decay, precision=lax.Precision.HIGHEST, preferred_element_type=f32)
        begin = sc_ref[starts] + j * SPAN
        doc_row = jnp.zeros((SPAN, SPAN), jnp.int32)
        doc_col = jnp.zeros((SPAN, SPAN), jnp.int32)
        doc_tok = jnp.zeros((SPAN, LANES), jnp.int32)
        token = lax.broadcasted_iota(jnp.int32, (SPAN, LANES), 0)
        doc_end = jnp.int32(0)
        for d in range(starts):
            at = sc_ref[d] - begin
            at = jnp.where(at < 0, SPAN, at)
            doc_row += (at <= row).astype(jnp.int32)
            doc_col += (at <= col).astype(jnp.int32)
            doc_tok += (at <= token).astype(jnp.int32)
            doc_end += (at < SPAN).astype(jnp.int32)
        linked = (doc_row == doc_col) & (col <= row)
        scores = lax.dot_general(
            q_ref[...], k_ref[...], (((1,), (1,)), ((), ())), preferred_element_type=f32
        )
        score_ref[0] = jnp.where(linked, scores, 0.0)
        last = cum[SPAN - 1 : SPAN, :]
        cum_ref[...] = cum
        rt_ref[0] = jnp.transpose(cum - jnp.log(step) * LOG2E)
        kt_ref[0] = jnp.transpose(k_ref[...].astype(f32)).astype(bf16)
        endw_ref[...] = jnp.where(doc_tok == doc_end, jnp.exp2(last - cum), 0.0) * step
        entry = jnp.where(doc_tok == 0, jnp.exp2(cum), 0.0)
        entry_ref[...] = entry
        entd_ref[...] = entry * pref[0:1, :]
        kept = jnp.where(doc_end == 0, jnp.exp2(last), 0.0)
        kept = jnp.broadcast_to(kept, (8, LANES))
        ret_ref[0] = kept
        pref[...] = pref[...] * kept
        thru_ref[...] = pref[...]

    block = columns // LANES
    span_rows = pl.BlockSpec((SPAN, LANES), lambda j, s: (j, 0))
    rows = jax.ShapeDtypeStruct((tokens, LANES), f32)
    return pl.pallas_call(
        kernel,
        out_shape=(
            rows,
            jax.ShapeDtypeStruct((spans, LANES, SPAN), f32),
            jax.ShapeDtypeStruct((spans, SPAN, SPAN), f32),
            jax.ShapeDtypeStruct((spans, LANES, SPAN), bf16),
            rows,
            rows,
            rows,
            jax.ShapeDtypeStruct((spans, 8, LANES), f32),
            jax.ShapeDtypeStruct((8, LANES), f32),
        ),
        grid_spec=pltpu.PrefetchScalarGridSpec(
            num_scalar_prefetch=1,
            grid=(spans,),
            in_specs=[
                pl.BlockSpec((SPAN, LANES), lambda j, s: (j, block)),
                pl.BlockSpec((SPAN, LANES), lambda j, s: (j, block + 1)),
                pl.BlockSpec((SPAN, LANES), lambda j, s: (j, block + 2)),
                pl.BlockSpec((1, LANES), lambda j, s: (0, 0)),
            ],
            out_specs=[
                span_rows,
                pl.BlockSpec((1, LANES, SPAN), lambda j, s: (j, 0, 0)),
                pl.BlockSpec((1, SPAN, SPAN), lambda j, s: (j, 0, 0)),
                pl.BlockSpec((1, LANES, SPAN), lambda j, s: (j, 0, 0)),
                span_rows,
                span_rows,
                span_rows,
                pl.BlockSpec((1, 8, LANES), lambda j, s: (j, 0, 0)),
                pl.BlockSpec((8, LANES), lambda j, s: (0, 0)),
            ],
            scratch_shapes=[pltpu.VMEM((8, LANES), f32)],
        ),
        compiler_params=params(56, "arbitrary"),
        cost_estimate=estimate(spans * 2 * SPAN * SPAN * LANES * 7, 6 * 2**20),
    )(scalars, packed, packed, packed, decay_row)


def spreader(width, head_width, first_head):
    lane = lax.broadcasted_iota(jnp.int32, (LANES, width), 1)
    start = (lax.broadcasted_iota(jnp.int32, (LANES, width), 0) - first_head) * head_width
    once = ((lane >= start) & (lane < start + head_width)).astype(f32).astype(bf16)
    return jnp.concatenate([once, once], axis=0)


def halves(x):
    high = x.astype(bf16)
    return high, (x - high.astype(f32)).astype(bf16)


def summands(table):
    return jnp.concatenate(halves(table), axis=1)


def spread(pair, matrix):
    return jnp.dot(pair, matrix, preferred_element_type=f32)


def blocks(
    got, slot, width, first_head, head_width, tables, aux, query_at, skip_row, result, whole_width, with_end, with_local
):
    cum, rt, scores, kt, endw, entry, _, ret, thru = tables
    tokens = slot.shape[0] * SEG
    spans = tokens // SPAN
    step_width = GROUP * head_width
    groups = width // step_width
    place = first_head * head_width // width
    half = SPAN // 2
    runs = SPAN // SEG
    in_order = got.ndim == 4
    hand_on = with_end and not with_local

    def kernel(slot_ref, *refs):
        refs = list(refs)
        got_ref, kt_ref, endw_ref, ret_ref, thru_ref = refs[:5]
        del refs[:5]
        if with_local:
            q_ref, cum_ref, rt_ref, score_ref, entry_ref, skip_ref = refs[:6]
            del refs[:6]
            if result is not None:
                del refs[:1]
        if with_end:
            final_ref = refs.pop(0)
        if hand_on:
            packed_ref, packed_sems = refs.pop(0), refs[-1]
        if with_local:
            out_ref = refs.pop(0)
            outs_held, out_sems = refs[-2:]
        state, matrix, held, sems = refs[:4]

        @pl.loop(0, spans)
        def _(j):
            if in_order:
                pltpu.make_async_copy(got_ref.at[j], held.at[j], sems.at[j]).start()
                return

            @pl.loop(0, runs, unroll=runs)
            def _(i):
                pltpu.make_async_copy(
                    got_ref.at[slot_ref[j * runs + i], :, pl.ds(0, width)], held.at[j, i], sems.at[j]
                ).start()

        state[...] = jnp.zeros_like(state)
        for g in range(groups):
            matrix[g] = spreader(step_width, head_width, first_head + g * GROUP)

        def written(j):
            return pltpu.make_async_copy(
                outs_held.at[lax.rem(j, 2)],
                out_ref.at[pl.ds(pl.multiple_of(j * SPAN, SPAN), SPAN), pl.ds(first_head * head_width, width)],
                out_sems.at[lax.rem(j, 2)],
            )

        @pl.loop(0, spans)
        def _(j):
            tokens_of = pl.ds(pl.multiple_of(j * SPAN, SPAN), SPAN)
            end_weight = summands(endw_ref[tokens_of, :])
            kept_all = summands(ret_ref[j])
            if with_local:
                entry_all = summands(entry_ref[tokens_of, :])
                query = q_ref[tokens_of, :]
                query = jnp.concatenate([query, query], axis=1)
                lane = lax.broadcasted_iota(jnp.int32, (half, 2 * head_width), 1)

                @pl.when(j >= 2)
                def _():
                    written(j - 2).wait()

            pltpu.make_async_copy(held.at[j], held.at[j], sems.at[j]).wait()
            if hand_on:
                pltpu.make_async_copy(held.at[j], packed_ref.at[j], packed_sems.at[j]).start()

            for g in range(groups):
                head = first_head + g * GROUP
                columns = slice(g * step_width, (g + 1) * step_width)
                block = held[j, :, :, columns].reshape(SPAN, step_width)
                old = state[:, columns]
                scaled = block.astype(f32) * spread(end_weight, matrix[g])
                added = jnp.dot(kt_ref[j], scaled.astype(bf16), preferred_element_type=f32)
                state[:, columns] = spread(kept_all, matrix[g])[0:1, :] * old + added
                if not with_local:
                    continue
                base = jnp.dot(
                    query, jnp.concatenate(halves(old), axis=0), preferred_element_type=f32
                )
                base = base * spread(entry_all, matrix[g])
                base = base + skip_ref[:, columns] * block.astype(f32)
                for pair in range(GROUP // 2):
                    at = pair * 2 * head_width
                    values = block[:, at : at + 2 * head_width]
                    for part in range(2):
                        reach = (part + 1) * half
                        rows = slice(part * half, reach)
                        rows_of = pl.ds(pl.multiple_of(j * SPAN + part * half, half), half)
                        outs = []
                        for h in (head + 2 * pair, head + 2 * pair + 1):
                            gap = cum_ref[rows_of, h : h + 1] - rt_ref[j, h : h + 1, 0:reach]
                            weights = score_ref[j, rows, 0:reach] * jnp.exp2(
                                jnp.minimum(gap, CEILING)
                            )
                            outs.append(
                                jnp.dot(
                                    weights.astype(bf16), values[0:reach], preferred_element_type=f32
                                )
                            )
                        within = jnp.where(lane < head_width, outs[0], outs[1])
                        to = columns.start + at
                        outs_held[lax.rem(j, 2), rows, to : to + 2 * head_width] = (
                            within + base[rows, at : at + 2 * head_width]
                        ).astype(bf16)
            if with_local:
                written(j).start()

        if with_end:
            through_all = summands(thru_ref[...])
            for g in range(groups):
                columns = slice(g * step_width, (g + 1) * step_width)
                final_ref[0:LANES, columns] = state[:, columns].astype(bf16)
                high, low = halves(spread(through_all, matrix[g]))
                final_ref[LANES : LANES + 16, columns] = jnp.concatenate([high, low], axis=0)
        if hand_on:

            @pl.loop(0, spans)
            def _(j):
                pltpu.make_async_copy(held.at[j], packed_ref.at[j], packed_sems.at[j]).wait()

        if with_local:
            for j in range(max(spans - 2, 0), spans):
                written(jnp.int32(j)).wait()

    def whole(array, columns=None, at=0):
        shape = array.shape if columns is None else array.shape[:-1] + (columns,)
        return pl.BlockSpec(shape, lambda i, s: (0,) * (len(shape) - 1) + (at,))

    anywhere = pl.BlockSpec(memory_space=pl.ANY)
    operands = [got, kt, endw, ret, thru]
    in_specs = [anywhere, whole(kt), whole(endw), whole(ret), whole(thru)]
    out_shape, out_specs, aliases = [], [], {}
    scratch = [
        pltpu.VMEM((LANES, width), f32),
        pltpu.VMEM((groups, 2 * LANES, step_width), bf16),
        pltpu.VMEM((spans, runs, SEG, width), bf16),
        pltpu.SemaphoreType.DMA((spans,)),
    ]
    if with_end:
        out_shape.append(jax.ShapeDtypeStruct((LANES + 16, width), bf16))
        out_specs.append(pl.BlockSpec((LANES + 16, width), lambda i, s: (0, 0)))
    if hand_on:
        out_shape.append(jax.ShapeDtypeStruct((spans, runs, SEG, width), bf16))
        out_specs.append(anywhere)
        scratch.append(pltpu.SemaphoreType.DMA((spans,)))
    if with_local:
        operands += [aux, cum, rt, scores, entry, skip_row]
        in_specs += [whole(aux, LANES, query_at), whole(cum), whole(rt), whole(scores), whole(entry)]
        in_specs.append(whole(skip_row, width, place))
        if result is not None:
            aliases = {1 + len(operands): len(out_shape)}
            operands.append(result)
            in_specs.append(anywhere)
        out_shape.append(jax.ShapeDtypeStruct((tokens, whole_width), bf16))
        out_specs.append(anywhere)
        scratch += [pltpu.VMEM((2, SPAN, width), bf16), pltpu.SemaphoreType.DMA((2,))]
    return pl.pallas_call(
        kernel,
        out_shape=tuple(out_shape),
        grid_spec=pltpu.PrefetchScalarGridSpec(
            num_scalar_prefetch=1,
            grid=(1,),
            in_specs=in_specs,
            out_specs=tuple(out_specs),
            scratch_shapes=scratch,
        ),
        input_output_aliases=aliases,
        compiler_params=params(56),
        cost_estimate=estimate(
            2 * tokens * width * (5 if with_local else 2) * SPAN,
            6 * tokens * width,
            tokens * SPAN * width // head_width if with_local else 0,
        ),
    )(slot, *operands)


def add_entering(result, width, first_head, head_width, query_at, aux, entd, arrived):
    tokens = result.shape[0]
    spans = tokens // SPAN
    step_width = GROUP * head_width
    groups = width // step_width

    def kernel(q_ref, entd_ref, *rest):
        froms = rest[: len(arrived)]
        in_ref, out_ref, matrix, state, held, in_sems, out_sems = rest[len(arrived) :]

        def place(ref, j):
            first = pl.multiple_of(j * SPAN, SPAN)
            return ref.at[pl.ds(first, SPAN), pl.ds(first_head * head_width, width)]

        @pl.loop(0, spans)
        def _(j):
            pltpu.make_async_copy(place(in_ref, j), held.at[j], in_sems.at[j]).start()

        for g in range(groups):
            matrix[g] = spreader(step_width, head_width, first_head + g * GROUP)
        incoming = froms[-1][0:LANES, :].astype(f32)
        for ref in reversed(froms[:-1]):
            factor = ref[LANES : LANES + 16, :].astype(f32)
            incoming = ref[0:LANES, :].astype(f32) + (factor[0:1, :] + factor[8:9, :]) * incoming
        state[...] = incoming.astype(bf16)

        @pl.loop(0, spans)
        def _(j):
            tokens_of = pl.ds(pl.multiple_of(j * SPAN, SPAN), SPAN)
            entry_all = summands(entd_ref[tokens_of, :])
            pltpu.make_async_copy(place(in_ref, j), held.at[j], in_sems.at[j]).wait()
            for g in range(groups):
                columns = slice(g * step_width, (g + 1) * step_width)
                part = jnp.dot(
                    q_ref[tokens_of, :], state[:, columns], preferred_element_type=f32
                )
                part = part * spread(entry_all, matrix[g])
                held[j, :, columns] = (held[j, :, columns].astype(f32) + part).astype(bf16)
            pltpu.make_async_copy(held.at[j], place(out_ref, j), out_sems.at[j]).start()

        @pl.loop(0, spans)
        def _(j):
            pltpu.make_async_copy(held.at[j], place(out_ref, j), out_sems.at[j]).wait()

    return pl.pallas_call(
        kernel,
        out_shape=jax.ShapeDtypeStruct(result.shape, result.dtype),
        grid=(1,),
        in_specs=[
            pl.BlockSpec((tokens, LANES), lambda i: (0, query_at)),
            pl.BlockSpec((tokens, LANES), lambda i: (0, 0)),
        ]
        + [pl.BlockSpec((LANES + 16, width), lambda i: (0, 0))] * len(arrived)
        + [pl.BlockSpec(memory_space=pl.ANY)],
        out_specs=pl.BlockSpec(memory_space=pl.ANY),
        scratch_shapes=[
            pltpu.VMEM((groups, 2 * LANES, step_width), bf16),
            pltpu.VMEM((LANES, width), bf16),
            pltpu.VMEM((spans, SPAN, width), bf16),
            pltpu.SemaphoreType.DMA((spans,)),
            pltpu.SemaphoreType.DMA((spans,)),
        ],
        input_output_aliases={2 + len(arrived): 0},
        compiler_params=params(56),
        cost_estimate=estimate(2 * tokens * width * 3 * LANES, 4 * tokens * width),
    )(aux, entd, *arrived, result)


def shifted(block, distance):
    count = lax.axis_size("seq")
    return lax.ppermute(block, "seq", [(i, i + distance) for i in range(count - distance)])


def on_device(
    token_rows, key_rows, query_rows, step_rows, decay_log, skip_gain, source_rows, document_starts
):
    tokens, whole_width = token_rows.shape
    peers = lax.axis_size("dp")
    shards = lax.axis_size("seq")
    heads = decay_log.shape[0]
    head_width = whole_width // heads
    runs = tokens // SEG
    capacity = runs // peers + 1

    first_rows = source_rows[0].reshape(runs, SEG)[:, 0]
    peer = first_rows // (tokens * shards)
    run = (first_rows % tokens) // SEG
    order = jnp.arange(runs)
    earlier = (peer[:, None] == peer[None, :]) & (order[None, :] < order[:, None])
    slot = peer * capacity + jnp.sum(earlier.astype(jnp.int32), axis=1)
    asked = jnp.sum(
        jnp.where(slot[None, :] == jnp.arange(peers * capacity)[:, None], run[None, :], 0), axis=1
    )
    wanted = lax.all_to_all(
        asked.reshape(peers, capacity), "dp", split_axis=0, concat_axis=0, tiled=True
    ).reshape(peers * capacity)

    aux_rows = side_rows(key_rows, query_rows, step_rows).reshape(runs, SEG, AUX)
    token_runs = token_rows.reshape(runs, SEG, whole_width)

    def exchange(block):
        rows = block.reshape(peers, capacity * SEG, block.shape[2])
        rows = lax.all_to_all(rows, "dp", split_axis=0, concat_axis=0, tiled=True)
        return rows.reshape(block.shape)

    widths = [n * head_width for n in PARTS]
    firsts = [sum(PARTS[:i]) for i in range(len(PARTS))]
    scalars = jnp.concatenate(
        [document_starts[0], (lax.axis_index("seq") * tokens).astype(jnp.int32)[None]]
    )
    decay_row = jnp.pad(decay_log, (0, LANES - heads))[None, :]
    skip_row = jnp.repeat(skip_gain, head_width)[None, :]
    query_at = 1
    parts = range(len(PARTS))

    sent = []
    for i in parts:
        sent.append(
            pick_runs(wanted, token_runs, firsts[i] * head_width, widths[i], None if i else aux_rows)
        )
        wanted, sent[i] = lax.optimization_barrier((wanted, sent[i]))
    got, arrived = [], []

    def work(i, result, with_end, with_local, rows=None):
        return blocks(
            got[i] if rows is None else rows, slot, widths[i], firsts[i], head_width, tables, aux, query_at, skip_row, result,
            whole_width, with_end, with_local,
        )

    def send_end(end):
        arrived.append([shifted(end, d) for d in range(1, shards)])

    def entering(i, result):
        return add_entering(
            result, widths[i], firsts[i], head_width, query_at, aux, tables[6], arrived[i]
        )

    got.append(exchange(sent[0]))
    got[0], sent[1] = lax.optimization_barrier((got[0], sent[1]))
    got.append(exchange(sent[1]))
    aux = pick_runs(slot, got[0], widths[0], AUX).reshape(tokens, AUX)
    tables = prepare(aux, 0, decay_row, scalars)
    end, result = work(0, None, True, True)
    send_end(end)
    result = entering(0, result)
    got[1], sent[2], result = lax.optimization_barrier((got[1], sent[2], result))
    got.append(exchange(sent[2]))
    end, rows = work(1, None, True, False)
    send_end(end)
    (result,) = work(1, result, False, True, rows)
    end, rows = work(2, None, True, False)
    send_end(end)
    (result,) = work(2, result, False, True, rows)
    result = entering(1, result)
    result = entering(2, result)
    return result[None]


def solution(mesh):
    in_specs = (
        P(("dp", "seq"), None),
        P(("dp", "seq"), None),
        P(("dp", "seq"), None),
        P(("dp", "seq"), None),
        P(),
        P(),
        P("dp", "seq"),
        P("dp", None),
    )
    out_specs = P("dp", "seq", None)
    return jax.shard_map(
        on_device, mesh=mesh, in_specs=in_specs, out_specs=out_specs, check_vma=False
    )
```
